128 devices in a mesh: dp: 8 (over y, core), tensor: 16 (over x, z).
Axes of the slice: x: 4, y: 4, z: 4, core: 2. Of those that a mesh axis runs over, the one named last changes fastest.
Arguments:
- queries: bfloat16 [64, 8192], P('dp', 'tensor'), may hold values from -100 to 100
- new_kv: bfloat16 [64, 16, 256], P('dp', 'tensor'), may hold values from -4 to 4, as said below
- kv_pages: bfloat16 [16, 512, 128, 256], P('tensor', 'dp'), may hold values from -4.1 to 4.1, as said below
- lengths: int32 [64], P('dp'), may hold values from 2 to 16384, as said below
- page_table: int32 [64, 128], P('dp'), may hold values from 0 to 511, as said below
- out_weight: bfloat16 [8192, 16384], P('tensor'), may hold values from -0.0625 to 0.0625
Outputs:
- projected: bfloat16 [64, 16384], P('dp', 'tensor')
The draws below stay inside these ranges and needn't reach their ends.
Inputs may be any that keep to these rules, and one draw needn't show every extreme that they name: `lengths`: one request in every draw has the longest context. `page_table`: page g is held by dp index g // 64. A request's entries before ceil(lengths / 128) name distinct pages, and no page is named by two requests; later entries are valid page numbers that carry no meaning. `kv_pages`: all copies of one key-value head are equal. `new_kv`: all copies of one key-value head are equal.
All inputs are finite; a program needn't handle non-finite values.
Results may differ from the reference program's by a relative error of at most 0.015.
Values may be sent and summed in bfloat16 or wider, within the bound.
No kernel may reach another device: no remote copies, remote signals or barrier semaphores. Data moves between devices by JAX's collectives and lax.ppermute only.
A program may use at most 192 MiB of HBM per device.

```python
import jax
import jax.numpy as jnp
from jax import lax

D = 16384
QUERY_HEADS = 64
KEY_VALUE_HEADS = 4
HEAD_SIZE = 128
PAGE_POSITIONS = 128
PAGE_LIST_SIZE = 128
REQUEST_TOTAL = 64
PAGE_TOTAL = 512
KEY_VALUE_COPIES = 16


def pool_layout(key):
    offset_start = jax.random.fold_in(key, 101)
    cut_key, long_key, tail_key, order_key = jax.random.split(offset_start, 4)
    budget = PAGE_TOTAL - PAGE_LIST_SIZE
    cuts = jnp.sort(jax.random.permutation(cut_key, budget - 1)[:REQUEST_TOTAL - 1] + 1).astype(jnp.int32)
    bounds = jnp.concatenate([jnp.zeros((1,), jnp.int32), cuts, jnp.full((1,), budget, jnp.int32)])
    pages = jnp.minimum(bounds[1:] - bounds[:-1], PAGE_LIST_SIZE)
    longest = jax.random.randint(long_key, (), 0, REQUEST_TOTAL)
    chosen = jnp.arange(REQUEST_TOTAL) == longest
    pages = jnp.where(chosen, PAGE_LIST_SIZE, pages)
    tails = jax.random.randint(tail_key, (REQUEST_TOTAL,), 2, PAGE_POSITIONS + 1)
    tails = jnp.where(chosen, PAGE_POSITIONS, tails)
    lengths = (pages - 1) * PAGE_POSITIONS + tails
    shuffled = jax.random.permutation(order_key, PAGE_TOTAL).astype(jnp.int32)
    order = (shuffled - shuffled[0] + PAGE_TOTAL - 1) % PAGE_TOTAL
    starts = jnp.cumsum(pages) - pages
    slot_rows = (starts[:, None] + jnp.arange(PAGE_LIST_SIZE)[None, :]) % PAGE_TOTAL
    table = order[slot_rows]
    return (lengths.astype(jnp.int32), table.astype(jnp.int32))


def cache_values(key):
    offset_start = jax.random.fold_in(key, 202)
    return jax.random.truncated_normal(offset_start, -4.0, 4.0, (KEY_VALUE_HEADS, PAGE_TOTAL, PAGE_POSITIONS, 2 * HEAD_SIZE), jnp.float32)


def draw_lengths(key, part):
    lengths, table = pool_layout(key)
    return lengths


def draw_page_table(key, part):
    lengths, table = pool_layout(key)
    return table


def draw_kv_pages(key, part):
    paged_cache = cache_values(key)
    return jnp.repeat(paged_cache, KEY_VALUE_COPIES // KEY_VALUE_HEADS, axis=0).astype(jnp.bfloat16)


def draw_queries(key, part):
    key = jax.random.fold_in(key, 5)
    drawn = 2.5 * jax.random.truncated_normal(key, -4.0, 4.0, (REQUEST_TOTAL, QUERY_HEADS, HEAD_SIZE), jnp.float32)
    return drawn.reshape(REQUEST_TOTAL, QUERY_HEADS * HEAD_SIZE).astype(jnp.bfloat16)


def draw_new_kv(key, part):
    key = jax.random.fold_in(key, 7)
    newest_rows = jax.random.truncated_normal(key, -4.0, 4.0, (REQUEST_TOTAL, KEY_VALUE_HEADS, 2 * HEAD_SIZE), jnp.float32)
    return jnp.repeat(newest_rows, KEY_VALUE_COPIES // KEY_VALUE_HEADS, axis=1).astype(jnp.bfloat16)


def shard_levels(rng, extent, cuts, low, top_value):
    loudness = 1.0
    for position, parts in cuts:
        heights = jax.random.uniform(jax.random.fold_in(jax.random.fold_in(rng, 6), position), (parts,), jnp.float32, low / len(cuts), top_value / len(cuts))
        loudness = loudness * jnp.repeat(jnp.exp(heights), extent[position] // parts).reshape((-1,) + (1,) * (len(extent) - 1 - position))
    return loudness


def noise(rng, extent, width, limit, shards=(), held_as=jnp.bfloat16):
    values = jax.random.normal(rng, extent, jnp.float32) * width
    if len(shards) > 0:
        values = shard_levels(rng, extent, shards, -0.22, 0.18) * values
    return jnp.clip(values, min=-limit, max=limit).astype(held_as)


def setup_inputs(seed: int = 0) -> dict:
    splits = jax.random.split(jax.random.key(seed), 7)
    return {
        "queries": draw_queries(jax.random.fold_in(splits[6], 71), 0),
        "new_kv": draw_new_kv(jax.random.fold_in(splits[6], 71), 0),
        "kv_pages": draw_kv_pages(jax.random.fold_in(splits[6], 71), 0),
        "lengths": draw_lengths(jax.random.fold_in(splits[6], 71), 0),
        "page_table": draw_page_table(jax.random.fold_in(splits[6], 71), 0),
        "out_weight": noise(splits[5], (QUERY_HEADS * HEAD_SIZE, D), (QUERY_HEADS * HEAD_SIZE) ** -0.5, 0.0625, ((0, 16),)),
    }


def reference(queries, new_kv, kv_pages, lengths, page_table, out_weight):
    head_copies = KEY_VALUE_COPIES // KEY_VALUE_HEADS
    request_group = QUERY_HEADS // KEY_VALUE_HEADS
    scaling = HEAD_SIZE ** -0.5
    key_value_heads = kv_pages[::head_copies]
    fresh_kv = new_kv[:, ::head_copies, :]
    positions = jnp.arange(PAGE_LIST_SIZE * PAGE_POSITIONS, dtype=jnp.int32).reshape(PAGE_LIST_SIZE, PAGE_POSITIONS)
    slots = jnp.arange(PAGE_LIST_SIZE, dtype=jnp.int32)

    def attend(operands):
        query_input, page_list_row, length, newest = operands
        collected_pages = jnp.take(key_value_heads, page_list_row, axis=1)
        key_rows = collected_pages[..., :HEAD_SIZE].astype(jnp.float32)
        value_rows = collected_pages[..., HEAD_SIZE:].astype(jnp.float32)
        query_matrix = query_input.astype(jnp.float32).reshape(KEY_VALUE_HEADS, request_group, HEAD_SIZE)
        scores = jnp.einsum('kgd,kptd->kgpt', query_matrix, key_rows) * scaling
        alive = (positions < length)[None, None]
        page_alive = (slots < (length + PAGE_POSITIONS - 1) // PAGE_POSITIONS)[None, None]
        page_peak = jnp.max(jnp.where(alive, scores, -jnp.inf), axis=-1)
        fresh = jnp.einsum('kgd,kd->kg', query_matrix, newest[:, :HEAD_SIZE].astype(jnp.float32)) * scaling
        peak = jnp.maximum(jnp.max(jnp.where(page_alive, page_peak, -jnp.inf), axis=-1), fresh)
        safe_peak = jnp.where(page_alive, page_peak, peak[:, :, None])
        local = jnp.where(alive, jnp.exp(scores - safe_peak[..., None]), 0.0)
        page_factor = jnp.where(page_alive, jnp.exp(safe_peak - peak[:, :, None]), 0.0)
        fresh_weight = jnp.exp(fresh - peak)
        total = jnp.sum(jnp.sum(local, axis=-1) * page_factor, axis=-1) + fresh_weight
        rounded = lax.optimization_barrier(local.astype(jnp.bfloat16))
        page_sums = jnp.einsum('kgpt,kptd->kgpd', rounded.astype(jnp.float32), value_rows)
        summed = jnp.einsum('kgpd,kgp->kgd', page_sums, page_factor)
        summed = summed + fresh_weight[:, :, None] * newest[:, None, HEAD_SIZE:].astype(jnp.float32)
        return (summed / total[:, :, None]).reshape(QUERY_HEADS * HEAD_SIZE).astype(jnp.bfloat16)

    attended = lax.map(attend, (queries, page_table, lengths, fresh_kv))
    return jnp.dot(attended, out_weight, preferred_element_type=jnp.float32).astype(jnp.bfloat16)
```

```python
import functools

import jax
import jax.numpy as jnp
from jax import lax
from jax.experimental import pallas as pl
from jax.experimental.pallas import tpu as pltpu
from jax.sharding import PartitionSpec as P

FAR_BELOW = -1e30
LANES = 128
F32 = jnp.float32
BF16 = jnp.bfloat16
NO_PAGE = 255.0
QUAD = 4


def iota(shape, axis):
    return lax.broadcasted_iota(jnp.int32, shape, axis)


def split3(x):
    high = x.astype(BF16).astype(F32)
    middle = (x - high).astype(BF16).astype(F32)
    return high, middle, x - high - middle


def attend_kernel(scaling, homes, asked_ref, kv_ref, out_ref, score_ref, value_ref):
    pages, page_len, width = kv_ref.shape
    head_dim = width // 2
    requests = asked_ref.shape[0]
    per_home = requests // homes
    heads = out_ref.shape[0] // requests
    rows = pages * heads
    q_width = heads * head_dim

    named = asked_ref[:, q_width : q_width + LANES].astype(F32)
    filled = asked_ref[:, q_width + LANES : q_width + 2 * LANES].astype(F32)
    coded = filled + iota(filled.shape, 0).astype(F32) * 256.0
    page_id = iota((pages, LANES), 0).astype(F32)
    found = jnp.zeros((pages, LANES), F32)
    for r in range(requests):
        found = jnp.where(named[r : r + 1, :] == page_id, coded[r : r + 1, :], found)
    code = jnp.broadcast_to(jnp.sum(found, axis=1, keepdims=True), (pages, LANES))
    owner = jnp.floor(code * (1.0 / 256.0))
    alive_rows = code - owner * 256.0

    spread = (iota((rows, pages), 0) // heads == iota((rows, pages), 1)).astype(BF16)
    both = jnp.concatenate([owner, alive_rows], axis=1).astype(BF16)
    wide = jnp.dot(spread, both, preferred_element_type=F32)
    row_owner = wide[:, :LANES]
    alive = iota((rows, page_len), 1).astype(F32) < wide[:, LANES:]

    picker = (row_owner[:, :requests] == iota((rows, requests), 1).astype(F32)).astype(BF16)
    picked = jnp.dot(picker, asked_ref[:, :q_width], preferred_element_type=F32)
    row_head = iota((rows, head_dim), 0) % heads
    query = picked[:, :head_dim]
    for h in range(1, heads):
        query = jnp.where(row_head == h, picked[:, h * head_dim : (h + 1) * head_dim], query)
    query = query.astype(BF16)

    group = QUAD * heads
    block = iota((group, LANES), 0) // heads
    for j in range(pages // QUAD):
        keys = kv_ref[j * QUAD : (j + 1) * QUAD, :, :head_dim].reshape(QUAD * page_len, head_dim)
        full = lax.dot_general(
            query[j * group : (j + 1) * group, :],
            keys,
            (((1,), (1,)), ((), ())),
            preferred_element_type=F32,
        )
        mine = full[:, :page_len]
        for g in range(1, QUAD):
            mine = jnp.where(block == g, full[:, g * page_len : (g + 1) * page_len], mine)
        score_ref[j * group : (j + 1) * group, :] = mine
    scores = jnp.where(alive, score_ref[...] * scaling, FAR_BELOW)

    column = iota((rows, requests * heads), 1)
    column_head = (column // per_home) % heads
    column_request = (column // (per_home * heads)) * per_home + column % per_home
    owner_wide = jnp.concatenate([row_owner] * (requests * heads // LANES), axis=1)
    belongs = (owner_wide == column_request.astype(F32)) & (
        iota((rows, requests * heads), 0) % heads == column_head
    )

    page_peak = jnp.max(scores, axis=1, keepdims=True)
    peak = jnp.max(jnp.where(belongs, page_peak, FAR_BELOW), axis=0, keepdims=True)
    shift = jnp.max(jnp.where(belongs, peak, FAR_BELOW), axis=1, keepdims=True)
    local = jnp.where(alive, jnp.exp(scores - shift), 0.0)
    page_total = jnp.sum(local, axis=1, keepdims=True)

    for j in range(pages // QUAD):
        part = local[j * group : (j + 1) * group, :]
        weights = jnp.concatenate(
            [jnp.where(block == g, part, 0.0) for g in range(QUAD)], axis=1
        ).astype(BF16)
        values = kv_ref[j * QUAD : (j + 1) * QUAD, :, head_dim:].reshape(QUAD * page_len, head_dim)
        value_ref[j * group : (j + 1) * group, :] = jnp.dot(
            weights, values, preferred_element_type=F32
        )
    both = jnp.concatenate(
        [value_ref[...], jnp.broadcast_to(page_total, (rows, LANES))], axis=1
    )
    high = both.astype(BF16)
    low = (both - high.astype(F32)).astype(BF16)
    chosen = jnp.where(belongs, 1.0, 0.0).T.astype(BF16)
    summed = jnp.dot(chosen, high, preferred_element_type=F32) + jnp.dot(
        chosen, low, preferred_element_type=F32
    )
    weighted, total = summed[:, :head_dim], summed[:, head_dim:]
    peak_rows = jnp.broadcast_to(peak, (LANES, requests * heads)).T
    present = total > 0.0
    safe = jnp.where(present, total, 1.0)
    level = jnp.where(present, peak_rows + jnp.log(safe), FAR_BELOW)
    lane = iota(level.shape, 1)
    high, middle, low = split3(level)
    pieces = jnp.where(lane == 0, high, jnp.where(lane == 1, middle, low))
    out_ref[:, :head_dim] = (weighted / safe).astype(BF16)
    out_ref[:, head_dim:] = pieces.astype(BF16)


def project_kernel(scaling, parts_ref, query_ref, newest_ref, weight_ref, out_ref, input_ref):
    sources, rows, width = parts_ref.shape
    head_dim = width // 2
    req, q_width = query_ref.shape
    heads = q_width // head_dim

    @pl.when(pl.program_id(0) == 0)
    def _():
        newest = newest_ref[...].astype(F32)
        new_key, new_value = newest[:, :head_dim], newest[:, head_dim:]
        query = query_ref[...].astype(F32)
        fresh = jnp.concatenate(
            [
                jnp.sum(
                    query[:, h * head_dim : (h + 1) * head_dim] * new_key, axis=1, keepdims=True
                )
                for h in range(heads)
            ],
            axis=0,
        ) * scaling
        levels = []
        for s in range(sources):
            pieces = parts_ref[s, :, head_dim:].astype(F32)
            levels.append(pieces[:, 0:1] + pieces[:, 1:2] + pieces[:, 2:3])
        peak = fresh
        for level in levels:
            peak = jnp.maximum(peak, level)
        total = jnp.exp(fresh - peak)
        summed = total * jnp.concatenate([new_value] * heads, axis=0)
        for s in range(sources):
            factor = jnp.exp(levels[s] - peak)
            total = total + factor
            summed = summed + factor * parts_ref[s, :, :head_dim].astype(F32)
        attended = summed / total
        for h in range(heads):
            input_ref[:, h * head_dim : (h + 1) * head_dim] = attended[
                h * req : (h + 1) * req, :
            ].astype(BF16)

    tile = jnp.dot(input_ref[...], weight_ref[...], preferred_element_type=F32).astype(BF16)
    width_out = out_ref.shape[2]
    for k in range(out_ref.shape[0]):
        out_ref[k] = tile[:, k * width_out : (k + 1) * width_out]


def body(n_dp, n_tensor, queries, new_kv, kv_pages, lengths, page_table, out_weight):
    req_home, q_width = queries.shape
    _, pool_home, page_len, width = kv_pages.shape
    head_dim = width // 2
    heads = q_width // head_dim
    list_len = page_table.shape[1]
    features = out_weight.shape[1]
    requests = req_home * n_dp
    scaling = head_dim ** (-0.5)

    slot = jnp.arange(list_len, dtype=jnp.int32)
    filled = jnp.clip(lengths[:, None] - slot[None, :] * page_len, 0, page_len)
    holder = jnp.arange(n_dp, dtype=jnp.int32)[:, None, None]
    inside = page_table[None] - holder * pool_home
    valid = (inside >= 0) & (inside < pool_home) & (filled > 0)[None]
    named = jnp.where(valid, inside.astype(F32), NO_PAGE).astype(BF16)
    asked = jnp.concatenate(
        [
            jnp.broadcast_to(queries[None], (n_dp, req_home, q_width)),
            named,
            jnp.broadcast_to(filled.astype(BF16)[None], (n_dp, req_home, list_len)),
        ],
        axis=2,
    )
    asked = lax.all_to_all(asked, "dp", 0, 0).reshape(requests, q_width + 2 * list_len)

    parts = pl.pallas_call(
        functools.partial(attend_kernel, scaling, n_dp),
        out_shape=jax.ShapeDtypeStruct((requests * heads, width), BF16),
        in_specs=[pl.BlockSpec(memory_space=pltpu.VMEM)] * 2,
        out_specs=pl.BlockSpec(memory_space=pltpu.VMEM),
        scratch_shapes=[
            pltpu.VMEM((pool_home * heads, page_len), F32),
            pltpu.VMEM((pool_home * heads, head_dim), F32),
        ],
        compiler_params=pltpu.CompilerParams(vmem_limit_bytes=16 * 2**20),
        name="attend",
    )(asked, kv_pages[0])

    parts = lax.all_to_all(parts.reshape(n_dp, req_home * heads, width), "dp", 0, 0)

    own = features // n_tensor
    step = 2
    partial_out = pl.pallas_call(
        functools.partial(project_kernel, scaling),
        grid=(n_tensor // step,),
        out_shape=jax.ShapeDtypeStruct((n_tensor, req_home, own), BF16),
        in_specs=[
            pl.BlockSpec(memory_space=pltpu.VMEM),
            pl.BlockSpec(memory_space=pltpu.VMEM),
            pl.BlockSpec(memory_space=pltpu.VMEM),
            pl.BlockSpec((q_width, step * own), lambda i: (0, i)),
        ],
        out_specs=pl.BlockSpec((step, req_home, own), lambda i: (i, 0, 0)),
        scratch_shapes=[pltpu.VMEM((req_home, q_width), BF16)],
        compiler_params=pltpu.CompilerParams(vmem_limit_bytes=16 * 2**20),
        name="project",
    )(parts, queries, new_kv[:, 0, :], out_weight)

    pieces = lax.all_to_all(partial_out, "tensor", 0, 0)
    return jnp.sum(pieces.astype(F32), axis=0).astype(BF16)


def solution(mesh):
    return jax.shard_map(
        functools.partial(body, mesh.shape["dp"], mesh.shape["tensor"]),
        mesh=mesh,
        in_specs=(
            P("dp", "tensor"),
            P("dp", "tensor", None),
            P("tensor", "dp", None, None),
            P("dp"),
            P("dp", None),
            P("tensor", None),
        ),
        out_specs=P("dp", "tensor"),
        check_vma=False,
    )
```

```python
import functools

import jax
import jax.numpy as jnp
from jax import lax
from jax.experimental import pallas as pl
from jax.experimental.pallas import tpu as pltpu
from jax.sharding import PartitionSpec as P

FAR_BELOW = -1e30
LANES = 128
F32 = jnp.float32
BF16 = jnp.bfloat16
NO_PAGE = 255.0
QUAD = 4


def iota(shape, axis):
    return lax.broadcasted_iota(jnp.int32, shape, axis)


def split3(x):
    high = x.astype(BF16).astype(F32)
    middle = (x - high).astype(BF16).astype(F32)
    return high, middle, x - high - middle


def begin_kernel(out_ref):
    out_ref[...] = jnp.zeros_like(out_ref)


def ask_kernel(
    scaling, pool, page_len, _, length_ref, query_ref, newest_ref, table_ref, asked_ref, state_ref
):
    homes, req, width = asked_ref.shape
    q_width = query_ref.shape[1]
    list_len = table_ref.shape[1]
    head_dim = newest_ref.shape[1] // 2
    heads = q_width // head_dim
    row = iota((req, list_len), 0)
    length = jnp.zeros((req, list_len), jnp.int32)
    for r in range(req):
        length = jnp.where(row == r, length_ref[r], length)
    filled = jnp.clip(length - iota((req, list_len), 1) * page_len, 0, page_len)
    table = table_ref[...]
    query = query_ref[...]
    for d in range(homes):
        inside = table - d * pool
        valid = (inside >= 0) & (inside < pool) & (filled > 0)
        asked_ref[d, :, :q_width] = query
        asked_ref[d, :, q_width : q_width + list_len] = jnp.where(
            valid, inside.astype(F32), NO_PAGE
        ).astype(BF16)
        asked_ref[d, :, q_width + list_len :] = filled.astype(F32).astype(BF16)
    newest = newest_ref[...].astype(F32)
    wide = query.astype(F32)
    for h in range(heads):
        fresh = jnp.sum(
            wide[:, h * head_dim : (h + 1) * head_dim] * newest[:, :head_dim],
            axis=1,
            keepdims=True,
        )
        state_ref[h * req : (h + 1) * req, :head_dim] = newest[:, head_dim:]
        state_ref[h * req : (h + 1) * req, head_dim:] = jnp.broadcast_to(
            fresh * scaling, (req, head_dim)
        )


def attend_kernel(scaling, homes, asked_ref, kv_ref, out_ref, score_ref, value_ref):
    pages, page_len, width = kv_ref.shape
    head_dim = width // 2
    requests = asked_ref.shape[0]
    per_home = requests // homes
    heads = out_ref.shape[0] // requests
    rows = pages * heads
    q_width = heads * head_dim

    named = asked_ref[:, q_width : q_width + LANES].astype(F32)
    filled = asked_ref[:, q_width + LANES : q_width + 2 * LANES].astype(F32)
    coded = filled + iota(filled.shape, 0).astype(F32) * 256.0
    page_id = iota((pages, LANES), 0).astype(F32)
    found = jnp.zeros((pages, LANES), F32)
    for r in range(requests):
        found = jnp.where(named[r : r + 1, :] == page_id, coded[r : r + 1, :], found)
    code = jnp.broadcast_to(jnp.sum(found, axis=1, keepdims=True), (pages, LANES))
    owner = jnp.floor(code * (1.0 / 256.0))
    alive_rows = code - owner * 256.0

    spread = (iota((rows, pages), 0) // heads == iota((rows, pages), 1)).astype(BF16)
    both = jnp.concatenate([owner, alive_rows], axis=1).astype(BF16)
    wide = jnp.dot(spread, both, preferred_element_type=F32)
    row_owner = wide[:, :LANES]
    alive = iota((rows, page_len), 1).astype(F32) < wide[:, LANES:]

    picker = (row_owner[:, :requests] == iota((rows, requests), 1).astype(F32)).astype(BF16)
    picked = jnp.dot(picker, asked_ref[:, :q_width], preferred_element_type=F32)
    row_head = iota((rows, head_dim), 0) % heads
    query = picked[:, :head_dim]
    for h in range(1, heads):
        query = jnp.where(row_head == h, picked[:, h * head_dim : (h + 1) * head_dim], query)
    query = query.astype(BF16)

    group = QUAD * heads
    block = iota((group, LANES), 0) // heads
    for j in range(pages // QUAD):
        keys = kv_ref[j * QUAD : (j + 1) * QUAD, :, :head_dim].reshape(QUAD * page_len, head_dim)
        full = lax.dot_general(
            query[j * group : (j + 1) * group, :],
            keys,
            (((1,), (1,)), ((), ())),
            preferred_element_type=F32,
        )
        mine = full[:, :page_len]
        for g in range(1, QUAD):
            mine = jnp.where(block == g, full[:, g * page_len : (g + 1) * page_len], mine)
        score_ref[j * group : (j + 1) * group, :] = mine
    scores = jnp.where(alive, score_ref[...] * scaling, FAR_BELOW)

    column = iota((rows, requests * heads), 1)
    column_head = (column // per_home) % heads
    column_request = (column // (per_home * heads)) * per_home + column % per_home
    owner_wide = jnp.concatenate([row_owner] * (requests * heads // LANES), axis=1)
    belongs = (owner_wide == column_request.astype(F32)) & (
        iota((rows, requests * heads), 0) % heads == column_head
    )

    page_peak = jnp.max(scores, axis=1, keepdims=True)
    peak = jnp.max(jnp.where(belongs, page_peak, FAR_BELOW), axis=0, keepdims=True)
    shift = jnp.max(jnp.where(belongs, peak, FAR_BELOW), axis=1, keepdims=True)
    local = jnp.where(alive, jnp.exp(scores - shift), 0.0)
    page_total = jnp.sum(local, axis=1, keepdims=True)

    for j in range(pages // QUAD):
        part = local[j * group : (j + 1) * group, :]
        weights = jnp.concatenate(
            [jnp.where(block == g, part, 0.0) for g in range(QUAD)], axis=1
        ).astype(BF16)
        values = kv_ref[j * QUAD : (j + 1) * QUAD, :, head_dim:].reshape(QUAD * page_len, head_dim)
        value_ref[j * group : (j + 1) * group, :] = jnp.dot(
            weights, values, preferred_element_type=F32
        )
    both = jnp.concatenate(
        [value_ref[...], jnp.broadcast_to(page_total, (rows, LANES))], axis=1
    )
    high = both.astype(BF16)
    low = (both - high.astype(F32)).astype(BF16)
    chosen = jnp.where(belongs, 1.0, 0.0).T.astype(BF16)
    summed = jnp.dot(chosen, high, preferred_element_type=F32) + jnp.dot(
        chosen, low, preferred_element_type=F32
    )
    weighted, total = summed[:, :head_dim], summed[:, head_dim:]
    peak_rows = jnp.broadcast_to(peak, (LANES, requests * heads)).T
    present = total > 0.0
    safe = jnp.where(present, total, 1.0)
    level = jnp.where(present, peak_rows + jnp.log(safe), FAR_BELOW)
    lane = iota(level.shape, 1)
    high, middle, low = split3(level)
    pieces = jnp.where(lane == 0, high, jnp.where(lane == 1, middle, low))
    out_ref[:, :head_dim] = (weighted / safe).astype(BF16)
    out_ref[:, head_dim:] = pieces.astype(BF16)


def project_kernel(parts_ref, state_ref, weight_ref, out_ref):
    sources, rows, width = parts_ref.shape
    head_dim = width // 2
    blocks, req, own = out_ref.shape
    heads = rows // req
    fresh = state_ref[:, head_dim : head_dim + 1]
    levels = []
    for s in range(sources):
        pieces = parts_ref[s, :, head_dim:].astype(F32)
        levels.append(pieces[:, 0:1] + pieces[:, 1:2] + pieces[:, 2:3])
    peak = fresh
    for level in levels:
        peak = jnp.maximum(peak, level)
    total = jnp.exp(fresh - peak)
    summed = total * state_ref[:, :head_dim]
    for s in range(sources):
        factor = jnp.exp(levels[s] - peak)
        total = total + factor
        summed = summed + factor * parts_ref[s, :, :head_dim].astype(F32)
    attended = summed / total
    given = jnp.concatenate(
        [attended[h * req : (h + 1) * req, :] for h in range(heads)], axis=1
    ).astype(BF16)
    for k in range(blocks):
        out_ref[k] = jnp.dot(
            given, weight_ref[:, k * own : (k + 1) * own], preferred_element_type=F32
        ).astype(BF16)


def body(n_dp, n_tensor, queries, new_kv, kv_pages, lengths, page_table, out_weight):
    req_home, q_width = queries.shape
    _, pool_home, page_len, width = kv_pages.shape
    head_dim = width // 2
    heads = q_width // head_dim
    list_len = page_table.shape[1]
    features = out_weight.shape[1]
    requests = req_home * n_dp
    scaling = head_dim ** (-0.5)

    vmem = pl.BlockSpec(memory_space=pltpu.VMEM)
    begun = pl.pallas_call(
        begin_kernel,
        out_shape=jax.ShapeDtypeStruct((8, LANES), jnp.int32),
        out_specs=vmem,
        compiler_params=pltpu.CompilerParams(vmem_limit_bytes=2**20),
        cost_estimate=pl.CostEstimate(flops=10**10, bytes_accessed=2**20, transcendentals=0),
        name="begin",
    )()
    asked, state = pl.pallas_call(
        functools.partial(ask_kernel, scaling, pool_home, page_len),
        out_shape=(
            jax.ShapeDtypeStruct((n_dp, req_home, q_width + 2 * list_len), BF16),
            jax.ShapeDtypeStruct((req_home * heads, width), F32),
        ),
        in_specs=[vmem, pl.BlockSpec(memory_space=pltpu.SMEM), vmem, vmem, vmem],
        out_specs=(vmem, vmem),
        compiler_params=pltpu.CompilerParams(vmem_limit_bytes=4 * 2**20),
        cost_estimate=pl.CostEstimate(flops=10**10, bytes_accessed=2**20, transcendentals=0),
        name="ask",
    )(begun, lengths, queries, new_kv[:, 0, :], page_table)
    asked = lax.all_to_all(asked, "dp", 0, 0).reshape(requests, q_width + 2 * list_len)

    parts = pl.pallas_call(
        functools.partial(attend_kernel, scaling, n_dp),
        out_shape=jax.ShapeDtypeStruct((requests * heads, width), BF16),
        in_specs=[vmem, vmem],
        out_specs=vmem,
        scratch_shapes=[
            pltpu.VMEM((pool_home * heads, page_len), F32),
            pltpu.VMEM((pool_home * heads, head_dim), F32),
        ],
        compiler_params=pltpu.CompilerParams(vmem_limit_bytes=12 * 2**20),
        cost_estimate=pl.CostEstimate(flops=10**10, bytes_accessed=2**22, transcendentals=0),
        name="attend",
    )(asked, kv_pages[0])

    parts = lax.all_to_all(parts.reshape(n_dp, req_home * heads, width), "dp", 0, 0)

    own = features // n_tensor
    partial_out = pl.pallas_call(
        project_kernel,
        out_shape=jax.ShapeDtypeStruct((n_tensor, req_home, own), BF16),
        in_specs=[vmem, vmem, vmem],
        out_specs=vmem,
        compiler_params=pltpu.CompilerParams(vmem_limit_bytes=24 * 2**20),
        cost_estimate=pl.CostEstimate(flops=10**9, bytes_accessed=2**24, transcendentals=0),
        name="project",
    )(parts, state, out_weight)

    pieces = lax.all_to_all(partial_out, "tensor", 0, 0)
    return jnp.sum(pieces.astype(F32), axis=0).astype(BF16)


def solution(mesh):
    return jax.shard_map(
        functools.partial(body, mesh.shape["dp"], mesh.shape["tensor"]),
        mesh=mesh,
        in_specs=(
            P("dp", "tensor"),
            P("dp", "tensor", None),
            P("tensor", "dp", None, None),
            P("dp"),
            P("dp", None),
            P("tensor", None),
        ),
        out_specs=P("dp", "tensor"),
        check_vma=False,
    )
```

```python
import functools

import jax
import jax.numpy as jnp
from jax import lax
from jax.experimental import pallas as pl
from jax.experimental.pallas import tpu as pltpu
from jax.sharding import PartitionSpec as P

FAR_BELOW = -1e30
LANES = 128
F32 = jnp.float32
BF16 = jnp.bfloat16
PAGE_SHIFT = 256
NO_PAGE = 1024.0
CORES = 2
GROUP = 8


def iota(shape, axis):
    return lax.broadcasted_iota(jnp.int32, shape, axis)


def begin_kernel(out_ref):
    out_ref[...] = jnp.zeros_like(out_ref)


def ask_kernel(
    scaling, page_len, _, length_ref, query_ref, newest_ref, table_ref, asked_ref, state_ref
):
    req, q_width = query_ref.shape
    list_len = table_ref.shape[1]
    head_dim = newest_ref.shape[1] // 2
    heads = q_width // head_dim
    length = jnp.broadcast_to(length_ref[...], (req, req))
    length = jnp.where(iota((req, req), 0) == iota((req, req), 1), length, 0).astype(F32)
    length = jnp.sum(length, axis=1, keepdims=True)
    first = (iota((req, list_len), 1) * page_len).astype(F32)
    query = query_ref[...]
    asked_ref[:, :q_width] = query
    asked_ref[:, q_width : q_width + list_len] = (
        (table_ref[...] - PAGE_SHIFT).astype(F32).astype(BF16)
    )
    asked_ref[:, q_width + list_len :] = jnp.clip(length - first, 0.0, float(page_len)).astype(BF16)
    newest = newest_ref[...].astype(F32)
    wide = query.astype(F32)
    fresh = jnp.zeros((req, LANES), F32)
    for h in range(heads):
        product = wide[:, h * head_dim : (h + 1) * head_dim] * newest[:, :head_dim]
        score = jnp.sum(product, axis=1, keepdims=True) * scaling
        fresh = jnp.where(iota((req, LANES), 1) == h, score, fresh)
    state_ref[:, :head_dim] = newest[:, head_dim:]
    state_ref[:, head_dim:] = fresh


def attend_kernel(scaling, heads, chip_ref, *refs):
    *other_refs, kv_ref, out_ref = refs
    asked_refs = (chip_ref, *other_refs)
    pages, page_len, width = kv_ref.shape
    head_dim = width // 2
    per_chip = chip_ref.shape[0]
    requests = per_chip * len(asked_refs)
    per_home = per_chip // CORES
    q_width = heads * head_dim

    page_id = iota((pages, LANES), 0).astype(F32) + (
        lax.axis_index("dp") * pages - PAGE_SHIFT
    ).astype(F32)
    found = jnp.zeros((pages, LANES), F32)
    for k, asked_ref in enumerate(asked_refs):
        filled = asked_ref[:, q_width + LANES : q_width + 2 * LANES].astype(F32)
        named = asked_ref[:, q_width : q_width + LANES].astype(F32)
        named = jnp.where(filled > 0.0, named, NO_PAGE)
        coded = filled + (iota(filled.shape, 0) + k * per_chip).astype(F32) * 256.0
        for r in range(per_chip):
            found = jnp.where(named[r : r + 1, :] == page_id, coded[r : r + 1, :], found)
    code = jnp.broadcast_to(jnp.sum(found, axis=1, keepdims=True), (pages, LANES))
    owner = jnp.floor(code * (1.0 / 256.0))
    alive = iota((pages, page_len), 1).astype(F32) < code - owner * 256.0
    owns = owner == iota((pages, LANES), 1).astype(F32)
    picker = jnp.where(owns, 1.0, 0.0)

    asked = jnp.concatenate([ref[:, :q_width] for ref in asked_refs], axis=0)
    picked = jnp.dot(picker[:, :requests].astype(BF16), asked, preferred_element_type=F32)
    query = [picked[:, h * head_dim : (h + 1) * head_dim] for h in range(heads)]

    member = iota((GROUP, LANES), 0)
    scores = [[] for _ in range(heads)]
    for j in range(pages // GROUP):
        here = slice(j * GROUP, (j + 1) * GROUP)
        keys = kv_ref[here, :, :head_dim].reshape(GROUP * page_len, head_dim)
        full = lax.dot_general(
            jnp.concatenate([query[h][here] for h in range(heads)], axis=0).astype(BF16),
            keys,
            (((1,), (1,)), ((), ())),
            preferred_element_type=F32,
        )
        for h in range(heads):
            rows = full[h * GROUP : (h + 1) * GROUP]
            mine = rows[:, :page_len]
            for g in range(1, GROUP):
                mine = jnp.where(member == g, rows[:, g * page_len : (g + 1) * page_len], mine)
            scores[h].append(mine)
    page_peak, page_total, local = [], [], []
    for h in range(heads):
        score = jnp.where(alive, jnp.concatenate(scores[h], axis=0) * scaling, FAR_BELOW)
        page_peak.append(jnp.max(score, axis=1, keepdims=True))
        local.append(jnp.where(alive, jnp.exp(score - page_peak[h]), 0.0))
        page_total.append(jnp.sum(local[h], axis=1, keepdims=True))
    values = [[] for _ in range(heads)]
    for j in range(pages // GROUP):
        here = slice(j * GROUP, (j + 1) * GROUP)
        weights = jnp.concatenate(
            [
                jnp.concatenate(
                    [jnp.where(member == g, local[h][here], 0.0) for g in range(GROUP)], axis=1
                )
                for h in range(heads)
            ],
            axis=0,
        ).astype(BF16)
        group_values = jnp.dot(
            weights,
            kv_ref[here, :, head_dim:].reshape(GROUP * page_len, head_dim),
            preferred_element_type=F32,
        )
        for h in range(heads):
            values[h].append(group_values[h * GROUP : (h + 1) * GROUP])

    points, totals, scaled = [], [], []
    for h in range(heads):
        peak = jnp.max(jnp.where(owns, page_peak[h], FAR_BELOW), axis=0, keepdims=True)
        point = peak.astype(BF16).astype(F32)
        shift = jnp.max(jnp.where(owns, point, FAR_BELOW), axis=1, keepdims=True)
        factor = jnp.exp(jnp.minimum(page_peak[h] - shift, 80.0))
        total = jnp.sum(jnp.where(owns, page_total[h] * factor, 0.0), axis=0, keepdims=True)
        points.append(point)
        totals.append(total)
        scaled.append(jnp.concatenate(values[h], axis=0) * factor)
    scaled = jnp.concatenate(scaled, axis=1)
    high = scaled.astype(BF16)
    low = (scaled - high.astype(F32)).astype(BF16)
    chosen = picker.T[:requests].astype(BF16)
    summed = jnp.dot(chosen, high, preferred_element_type=F32) + jnp.dot(
        chosen, low, preferred_element_type=F32
    )
    summed = summed.astype(BF16)
    high = [total.astype(BF16).astype(F32) for total in totals]
    low = [total - part for total, part in zip(totals, high)]
    points = jnp.concatenate(points + points, axis=0).T
    totals = jnp.concatenate(high + low, axis=0).T
    wide = jnp.zeros((requests, LANES - 2 * heads), F32)
    points = jnp.concatenate([points[:requests], wide], axis=1)
    totals = jnp.concatenate([totals[:requests], wide], axis=1)
    for g in range(requests // per_home):
        home = lax.axis_index("dp") ^ g
        here = slice(g * per_home, (g + 1) * per_home)
        block = [summed[here, h * head_dim : (h + 1) * head_dim] for h in range(heads)]
        out_ref[home] = jnp.concatenate(
            block + [points[here].astype(BF16), totals[here].astype(BF16)], axis=0
        )


def project_kernel(part_ref, state_ref, weight_ref, out_ref):
    sources, rows, head_dim = part_ref.shape
    blocks, req, own = out_ref.shape
    heads = rows // req - 2
    fresh = state_ref[:, head_dim:]
    points = [part_ref[s, heads * req :, :].astype(F32)[:req] for s in range(sources)]
    peak = fresh
    for point in points:
        peak = jnp.maximum(peak, point)
    weight = jnp.exp(fresh - peak)
    total = weight
    summed = [weight[:, h : h + 1] * state_ref[:, :head_dim] for h in range(heads)]
    for s in range(sources):
        factor = jnp.exp(points[s] - peak)
        addends = part_ref[s, heads * req :, :].astype(F32)[req:]
        total = total + factor * (addends + pltpu.roll(addends, LANES - heads, 1))
        for h in range(heads):
            value = part_ref[s, h * req : (h + 1) * req, :].astype(F32)
            summed[h] = summed[h] + factor[:, h : h + 1] * value
    given = jnp.concatenate(
        [summed[h] / total[:, h : h + 1] for h in range(heads)], axis=1
    ).astype(BF16)
    for k in range(blocks):
        out_ref[k] = jnp.dot(
            given, weight_ref[:, k * own : (k + 1) * own], preferred_element_type=F32
        ).astype(BF16)


def body(n_dp, n_tensor, queries, new_kv, kv_pages, lengths, page_table, out_weight):
    req_home, q_width = queries.shape
    _, pool_home, page_len, width = kv_pages.shape
    head_dim = width // 2
    heads = q_width // head_dim
    list_len = page_table.shape[1]
    features = out_weight.shape[1]
    requests = req_home * n_dp
    scaling = head_dim ** (-0.5)

    vmem = pl.BlockSpec(memory_space=pltpu.VMEM)
    def swap(x, mask):
        return lax.ppermute(x, "dp", [(i, i ^ mask) for i in range(n_dp)])

    begun = pl.pallas_call(
        begin_kernel,
        out_shape=jax.ShapeDtypeStruct((8, LANES), jnp.int32),
        out_specs=vmem,
        compiler_params=pltpu.CompilerParams(vmem_limit_bytes=2**20),
        cost_estimate=pl.CostEstimate(flops=10**10, bytes_accessed=2**20, transcendentals=0),
        name="begin",
    )()
    asked, state = pl.pallas_call(
        functools.partial(ask_kernel, scaling, page_len),
        out_shape=(
            jax.ShapeDtypeStruct((req_home, q_width + 2 * list_len), BF16),
            jax.ShapeDtypeStruct((req_home, width), F32),
        ),
        in_specs=[vmem] * 5,
        out_specs=(vmem, vmem),
        compiler_params=pltpu.CompilerParams(vmem_limit_bytes=4 * 2**20),
        cost_estimate=pl.CostEstimate(flops=10**10, bytes_accessed=2**20, transcendentals=0),
        name="ask",
    )(begun, lengths.reshape(1, req_home), queries, new_kv[:, 0, :], page_table)
    asked = jnp.concatenate([asked, swap(asked, 1)], axis=0)
    chips = n_dp // CORES
    others = [swap(asked, CORES * k) for k in range(1, chips)]
    parts = pl.pallas_call(
        functools.partial(attend_kernel, scaling, heads),
        out_shape=jax.ShapeDtypeStruct((n_dp, req_home * (heads + 2), head_dim), BF16),
        in_specs=[vmem] * (chips + 1),
        out_specs=vmem,
        compiler_params=pltpu.CompilerParams(vmem_limit_bytes=12 * 2**20),
        cost_estimate=pl.CostEstimate(flops=10**10, bytes_accessed=2**22, transcendentals=0),
        name="attend",
    )(asked, *others, kv_pages[0])
    parts = lax.all_to_all(parts, "dp", 0, 0)

    own = features // n_tensor
    partial_out = pl.pallas_call(
        project_kernel,
        out_shape=jax.ShapeDtypeStruct((n_tensor, req_home, own), BF16),
        in_specs=[vmem] * 3,
        out_specs=vmem,
        compiler_params=pltpu.CompilerParams(vmem_limit_bytes=24 * 2**20),
        cost_estimate=pl.CostEstimate(flops=10**9, bytes_accessed=2**24, transcendentals=0),
        name="project",
    )(parts, state, out_weight)

    pieces = lax.all_to_all(partial_out, "tensor", 0, 0)
    return jnp.sum(pieces.astype(F32), axis=0).astype(BF16)


def solution(mesh):
    return jax.shard_map(
        functools.partial(body, mesh.shape["dp"], mesh.shape["tensor"]),
        mesh=mesh,
        in_specs=(
            P("dp", "tensor"),
            P("dp", "tensor", None),
            P("tensor", "dp", None, None),
            P("dp"),
            P("dp", None),
            P("tensor", None),
        ),
        out_specs=P("dp", "tensor"),
        check_vma=False,
    )
```

```python
import functools

import jax
import jax.numpy as jnp
from jax import lax
from jax.experimental import pallas as pl
from jax.experimental.pallas import tpu as pltpu
from jax.sharding import PartitionSpec as P

FAR_BELOW = -1e30
LANES = 128
F32 = jnp.float32
BF16 = jnp.bfloat16
PAGE_SHIFT = 256
NO_PAGE = 1024.0
CORES = 2
GROUP = 8


def iota(shape, axis):
    return lax.broadcasted_iota(jnp.int32, shape, axis)


def begin_kernel(out_ref):
    out_ref[...] = jnp.zeros_like(out_ref)


def ask_kernel(
    scaling, page_len, _, length_ref, query_ref, newest_ref, table_ref, asked_ref, state_ref
):
    req, q_width = query_ref.shape
    list_len = table_ref.shape[1]
    head_dim = newest_ref.shape[1] // 2
    heads = q_width // head_dim
    length = jnp.broadcast_to(length_ref[...], (req, req))
    length = jnp.where(iota((req, req), 0) == iota((req, req), 1), length, 0).astype(F32)
    length = jnp.sum(length, axis=1, keepdims=True)
    first = (iota((req, list_len), 1) * page_len).astype(F32)
    query = query_ref[...]
    named = (table_ref[...] - PAGE_SHIFT).astype(F32).astype(BF16)
    filled = jnp.clip(length - first, 0.0, float(page_len)).astype(BF16)
    for d in range(asked_ref.shape[0]):
        asked_ref[d, :, :q_width] = query
        asked_ref[d, :, q_width : q_width + list_len] = named
        asked_ref[d, :, q_width + list_len :] = filled
    newest = newest_ref[...].astype(F32)
    wide = query.astype(F32)
    fresh = jnp.zeros((req, LANES), F32)
    for h in range(heads):
        product = wide[:, h * head_dim : (h + 1) * head_dim] * newest[:, :head_dim]
        score = jnp.sum(product, axis=1, keepdims=True) * scaling
        fresh = jnp.where(iota((req, LANES), 1) == h, score, fresh)
    state_ref[:, :head_dim] = newest[:, head_dim:]
    state_ref[:, head_dim:] = fresh


def attend_kernel(scaling, homes, heads, chip_ref, *refs):
    *other_refs, kv_ref, out_ref = refs
    asked_refs = (chip_ref, *other_refs)
    pages, page_len, width = kv_ref.shape
    head_dim = width // 2
    per_chip = chip_ref.shape[0]
    requests = per_chip * len(asked_refs)
    per_home = requests // homes
    q_width = heads * head_dim

    page_id = iota((pages, LANES), 0).astype(F32) + (
        lax.axis_index("dp") * pages - PAGE_SHIFT
    ).astype(F32)
    found = jnp.zeros((pages, LANES), F32)
    for k, asked_ref in enumerate(asked_refs):
        filled = asked_ref[:, q_width + LANES : q_width + 2 * LANES].astype(F32)
        named = asked_ref[:, q_width : q_width + LANES].astype(F32)
        named = jnp.where(filled > 0.0, named, NO_PAGE)
        coded = filled + (iota(filled.shape, 0) + k * per_chip).astype(F32) * 256.0
        for r in range(per_chip):
            found = jnp.where(named[r : r + 1, :] == page_id, coded[r : r + 1, :], found)
    code = jnp.broadcast_to(jnp.sum(found, axis=1, keepdims=True), (pages, LANES))
    owner = jnp.floor(code * (1.0 / 256.0))
    alive = iota((pages, page_len), 1).astype(F32) < code - owner * 256.0
    owns = owner == iota((pages, LANES), 1).astype(F32)
    picker = jnp.where(owns, 1.0, 0.0)

    asked = jnp.concatenate([ref[:, :q_width] for ref in asked_refs], axis=0)
    picked = jnp.dot(picker[:, :requests].astype(BF16), asked, preferred_element_type=F32)
    query = [picked[:, h * head_dim : (h + 1) * head_dim] for h in range(heads)]

    member = iota((GROUP, LANES), 0)
    scores = [[] for _ in range(heads)]
    for j in range(pages // GROUP):
        here = slice(j * GROUP, (j + 1) * GROUP)
        keys = kv_ref[here, :, :head_dim].reshape(GROUP * page_len, head_dim)
        full = lax.dot_general(
            jnp.concatenate([query[h][here] for h in range(heads)], axis=0).astype(BF16),
            keys,
            (((1,), (1,)), ((), ())),
            preferred_element_type=F32,
        )
        for h in range(heads):
            rows = full[h * GROUP : (h + 1) * GROUP]
            mine = rows[:, :page_len]
            for g in range(1, GROUP):
                mine = jnp.where(member == g, rows[:, g * page_len : (g + 1) * page_len], mine)
            scores[h].append(mine)
    page_peak, page_total, local = [], [], []
    for h in range(heads):
        score = jnp.where(alive, jnp.concatenate(scores[h], axis=0) * scaling, FAR_BELOW)
        page_peak.append(jnp.max(score, axis=1, keepdims=True))
        local.append(jnp.where(alive, jnp.exp(score - page_peak[h]), 0.0))
        page_total.append(jnp.sum(local[h], axis=1, keepdims=True))
    values = [[] for _ in range(heads)]
    for j in range(pages // GROUP):
        here = slice(j * GROUP, (j + 1) * GROUP)
        weights = jnp.concatenate(
            [
                jnp.concatenate(
                    [jnp.where(member == g, local[h][here], 0.0) for g in range(GROUP)], axis=1
                )
                for h in range(heads)
            ],
            axis=0,
        ).astype(BF16)
        group_values = jnp.dot(
            weights,
            kv_ref[here, :, head_dim:].reshape(GROUP * page_len, head_dim),
            preferred_element_type=F32,
        )
        for h in range(heads):
            values[h].append(group_values[h * GROUP : (h + 1) * GROUP])

    points, totals, scaled = [], [], []
    for h in range(heads):
        peak = jnp.max(jnp.where(owns, page_peak[h], FAR_BELOW), axis=0, keepdims=True)
        point = peak.astype(BF16).astype(F32)
        shift = jnp.max(jnp.where(owns, point, FAR_BELOW), axis=1, keepdims=True)
        factor = jnp.exp(jnp.minimum(page_peak[h] - shift, 80.0))
        total = jnp.sum(jnp.where(owns, page_total[h] * factor, 0.0), axis=0, keepdims=True)
        points.append(point)
        totals.append(total)
        scaled.append(jnp.concatenate(values[h], axis=0) * factor)
    scaled = jnp.concatenate(scaled, axis=1)
    high = scaled.astype(BF16)
    low = (scaled - high.astype(F32)).astype(BF16)
    chosen = picker.T[:requests].astype(BF16)
    summed = jnp.dot(chosen, high, preferred_element_type=F32) + jnp.dot(
        chosen, low, preferred_element_type=F32
    )
    summed = summed.astype(BF16)
    high = [total.astype(BF16).astype(F32) for total in totals]
    low = [total - part for total, part in zip(totals, high)]
    points = jnp.concatenate(points + points, axis=0).T
    totals = jnp.concatenate(high + low, axis=0).T
    wide = jnp.zeros((requests, LANES - 2 * heads), F32)
    points = jnp.concatenate([points[:requests], wide], axis=1)
    totals = jnp.concatenate([totals[:requests], wide], axis=1)
    for g in range(requests // per_home):
        here = slice(g * per_home, (g + 1) * per_home)
        block = [summed[here, h * head_dim : (h + 1) * head_dim] for h in range(heads)]
        out_ref[g] = jnp.concatenate(
            block + [points[here].astype(BF16), totals[here].astype(BF16)], axis=0
        )


def project_kernel(part_ref, state_ref, weight_ref, out_ref):
    sources, rows, head_dim = part_ref.shape
    blocks, req, own = out_ref.shape
    heads = rows // req - 2
    fresh = state_ref[:, head_dim:]
    points = [part_ref[s, heads * req :, :].astype(F32)[:req] for s in range(sources)]
    peak = fresh
    for point in points:
        peak = jnp.maximum(peak, point)
    weight = jnp.exp(fresh - peak)
    total = weight
    summed = [weight[:, h : h + 1] * state_ref[:, :head_dim] for h in range(heads)]
    for s in range(sources):
        factor = jnp.exp(points[s] - peak)
        addends = part_ref[s, heads * req :, :].astype(F32)[req:]
        total = total + factor * (addends + pltpu.roll(addends, LANES - heads, 1))
        for h in range(heads):
            value = part_ref[s, h * req : (h + 1) * req, :].astype(F32)
            summed[h] = summed[h] + factor[:, h : h + 1] * value
    given = jnp.concatenate(
        [summed[h] / total[:, h : h + 1] for h in range(heads)], axis=1
    ).astype(BF16)
    for k in range(blocks):
        out_ref[k] = jnp.dot(
            given, weight_ref[:, k * own : (k + 1) * own], preferred_element_type=F32
        ).astype(BF16)


def body(n_dp, n_tensor, queries, new_kv, kv_pages, lengths, page_table, out_weight):
    req_home, q_width = queries.shape
    _, pool_home, page_len, width = kv_pages.shape
    head_dim = width // 2
    heads = q_width // head_dim
    list_len = page_table.shape[1]
    features = out_weight.shape[1]
    requests = req_home * n_dp
    scaling = head_dim ** (-0.5)

    vmem = pl.BlockSpec(memory_space=pltpu.VMEM)
    begun = pl.pallas_call(
        begin_kernel,
        out_shape=jax.ShapeDtypeStruct((8, LANES), jnp.int32),
        out_specs=vmem,
        compiler_params=pltpu.CompilerParams(vmem_limit_bytes=2**20),
        cost_estimate=pl.CostEstimate(flops=10**10, bytes_accessed=2**20, transcendentals=0),
        name="begin",
    )()
    asked, state = pl.pallas_call(
        functools.partial(ask_kernel, scaling, page_len),
        out_shape=(
            jax.ShapeDtypeStruct((n_dp, req_home, q_width + 2 * list_len), BF16),
            jax.ShapeDtypeStruct((req_home, width), F32),
        ),
        in_specs=[vmem] * 5,
        out_specs=(vmem, vmem),
        compiler_params=pltpu.CompilerParams(vmem_limit_bytes=4 * 2**20),
        cost_estimate=pl.CostEstimate(flops=10**11, bytes_accessed=2**20, transcendentals=0),
        name="ask",
    )(begun, lengths.reshape(1, req_home), queries, new_kv[:, 0, :], page_table)
    asked = lax.all_to_all(asked, "dp", 0, 0).reshape(requests, q_width + 2 * list_len)
    parts = pl.pallas_call(
        functools.partial(attend_kernel, scaling, n_dp, heads),
        out_shape=jax.ShapeDtypeStruct((n_dp, req_home * (heads + 2), head_dim), BF16),
        in_specs=[vmem] * 2,
        out_specs=vmem,
        compiler_params=pltpu.CompilerParams(vmem_limit_bytes=12 * 2**20),
        cost_estimate=pl.CostEstimate(flops=10**10, bytes_accessed=2**22, transcendentals=0),
        name="attend",
    )(asked, kv_pages[0])
    parts = lax.all_to_all(parts, "dp", 0, 0)

    own = features // n_tensor
    partial_out = pl.pallas_call(
        project_kernel,
        out_shape=jax.ShapeDtypeStruct((n_tensor, req_home, own), BF16),
        in_specs=[vmem] * 3,
        out_specs=vmem,
        compiler_params=pltpu.CompilerParams(vmem_limit_bytes=24 * 2**20),
        cost_estimate=pl.CostEstimate(flops=10**9, bytes_accessed=2**24, transcendentals=0),
        name="project",
    )(parts, state, out_weight)

    pieces = lax.all_to_all(partial_out, "tensor", 0, 0)
    return jnp.sum(pieces.astype(F32), axis=0).astype(BF16)


def solution(mesh):
    return jax.shard_map(
        functools.partial(body, mesh.shape["dp"], mesh.shape["tensor"]),
        mesh=mesh,
        in_specs=(
            P("dp", "tensor"),
            P("dp", "tensor", None),
            P("tensor", "dp", None, None),
            P("dp"),
            P("dp", None),
            P("tensor", None),
        ),
        out_specs=P("dp", "tensor"),
        check_vma=False,
    )
```

```python
import functools

import jax
import jax.numpy as jnp
from jax import lax
from jax.experimental import pallas as pl
from jax.experimental.pallas import tpu as pltpu
from jax.sharding import PartitionSpec as P

FAR_BELOW = -1e30
LANES = 128
F32 = jnp.float32
BF16 = jnp.bfloat16
PAGE_SHIFT = 256
NO_PAGE = 1024.0
CORES = 2
GROUP = 8


def iota(shape, axis):
    return lax.broadcasted_iota(jnp.int32, shape, axis)


def begin_kernel(out_ref):
    out_ref[...] = jnp.zeros_like(out_ref)


def ask_kernel(
    scaling, page_len, _, length_ref, query_ref, newest_ref, table_ref, asked_ref, state_ref
):
    req, q_width = query_ref.shape
    list_len = table_ref.shape[1]
    head_dim = newest_ref.shape[1] // 2
    heads = q_width // head_dim
    length = jnp.broadcast_to(length_ref[...], (req, req))
    length = jnp.where(iota((req, req), 0) == iota((req, req), 1), length, 0).astype(F32)
    length = jnp.sum(length, axis=1, keepdims=True)
    first = (iota((req, list_len), 1) * page_len).astype(F32)
    query = query_ref[...]
    named = (table_ref[...] - PAGE_SHIFT).astype(F32).astype(BF16)
    filled = jnp.clip(length - first, 0.0, float(page_len)).astype(BF16)
    for d in range(asked_ref.shape[0]):
        asked_ref[d, :, :q_width] = query
        asked_ref[d, :, q_width : q_width + list_len] = named
        asked_ref[d, :, q_width + list_len :] = filled
    newest = newest_ref[...].astype(F32)
    wide = query.astype(F32)
    fresh = jnp.zeros((req, LANES), F32)
    for h in range(heads):
        product = wide[:, h * head_dim : (h + 1) * head_dim] * newest[:, :head_dim]
        score = jnp.sum(product, axis=1, keepdims=True) * scaling
        fresh = jnp.where(iota((req, LANES), 1) == h, score, fresh)
    state_ref[:, :head_dim] = newest[:, head_dim:]
    state_ref[:, head_dim:] = fresh


def attend_kernel(scaling, homes, heads, chip_ref, *refs):
    *other_refs, kv_ref, out_ref = refs
    asked_refs = (chip_ref, *other_refs)
    pages, page_len, width = kv_ref.shape
    head_dim = width // 2
    per_chip = chip_ref.shape[0]
    requests = per_chip * len(asked_refs)
    per_home = requests // homes
    q_width = heads * head_dim

    page_id = iota((pages, LANES), 0).astype(F32) + (
        lax.axis_index("dp") * pages - PAGE_SHIFT
    ).astype(F32)
    found = jnp.zeros((pages, LANES), F32)
    for k, asked_ref in enumerate(asked_refs):
        filled = asked_ref[:, q_width + LANES : q_width + 2 * LANES].astype(F32)
        named = asked_ref[:, q_width : q_width + LANES].astype(F32)
        named = jnp.where(filled > 0.0, named, NO_PAGE)
        coded = filled + (iota(filled.shape, 0) + k * per_chip).astype(F32) * 256.0
        for r in range(per_chip):
            found = jnp.where(named[r : r + 1, :] == page_id, coded[r : r + 1, :], found)
    code = jnp.broadcast_to(jnp.sum(found, axis=1, keepdims=True), (pages, LANES))
    owner = jnp.floor(code * (1.0 / 256.0))
    alive = iota((pages, page_len), 1).astype(F32) < code - owner * 256.0
    owns = owner == iota((pages, LANES), 1).astype(F32)
    picker = jnp.where(owns, 1.0, 0.0)

    asked = jnp.concatenate([ref[:, :q_width] for ref in asked_refs], axis=0)
    picked = jnp.dot(picker[:, :requests].astype(BF16), asked, preferred_element_type=F32)
    query = [picked[:, h * head_dim : (h + 1) * head_dim] for h in range(heads)]

    member = iota((GROUP, LANES), 0)
    scores = [[] for _ in range(heads)]
    for j in range(pages // GROUP):
        here = slice(j * GROUP, (j + 1) * GROUP)
        keys = kv_ref[here, :, :head_dim].reshape(GROUP * page_len, head_dim)
        full = lax.dot_general(
            jnp.concatenate([query[h][here] for h in range(heads)], axis=0).astype(BF16),
            keys,
            (((1,), (1,)), ((), ())),
            preferred_element_type=F32,
        )
        for h in range(heads):
            rows = full[h * GROUP : (h + 1) * GROUP]
            mine = rows[:, :page_len]
            for g in range(1, GROUP):
                mine = jnp.where(member == g, rows[:, g * page_len : (g + 1) * page_len], mine)
            scores[h].append(mine)
    page_peak, page_total, local = [], [], []
    for h in range(heads):
        score = jnp.where(alive, jnp.concatenate(scores[h], axis=0) * scaling, FAR_BELOW)
        page_peak.append(jnp.max(score, axis=1, keepdims=True))
        local.append(jnp.where(alive, jnp.exp(score - page_peak[h]), 0.0))
        page_total.append(jnp.sum(local[h], axis=1, keepdims=True))
    values = [[] for _ in range(heads)]
    for j in range(pages // GROUP):
        here = slice(j * GROUP, (j + 1) * GROUP)
        weights = jnp.concatenate(
            [
                jnp.concatenate(
                    [jnp.where(member == g, local[h][here], 0.0) for g in range(GROUP)], axis=1
                )
                for h in range(heads)
            ],
            axis=0,
        ).astype(BF16)
        group_values = jnp.dot(
            weights,
            kv_ref[here, :, head_dim:].reshape(GROUP * page_len, head_dim),
            preferred_element_type=F32,
        )
        for h in range(heads):
            values[h].append(group_values[h * GROUP : (h + 1) * GROUP])

    points, totals, scaled = [], [], []
    for h in range(heads):
        peak = jnp.max(jnp.where(owns, page_peak[h], FAR_BELOW), axis=0, keepdims=True)
        point = peak.astype(BF16).astype(F32)
        shift = jnp.max(jnp.where(owns, point, FAR_BELOW), axis=1, keepdims=True)
        factor = jnp.exp(jnp.minimum(page_peak[h] - shift, 80.0))
        total = jnp.sum(jnp.where(owns, page_total[h] * factor, 0.0), axis=0, keepdims=True)
        points.append(point)
        totals.append(total)
        scaled.append(jnp.concatenate(values[h], axis=0) * factor)
    scaled = jnp.concatenate(scaled, axis=1)
    high = scaled.astype(BF16)
    low = (scaled - high.astype(F32)).astype(BF16)
    chosen = picker.T[:requests].astype(BF16)
    summed = jnp.dot(chosen, high, preferred_element_type=F32) + jnp.dot(
        chosen, low, preferred_element_type=F32
    )
    high = [total.astype(BF16).astype(F32) for total in totals]
    low = [total - part for total, part in zip(totals, high)]
    marks = jnp.concatenate(points + high + low + low, axis=0).T[:requests]
    marks = jnp.concatenate([marks, jnp.zeros((requests, LANES - 4 * heads), F32)], axis=1)
    for g in range(requests // per_home):
        here = slice(g * per_home, (g + 1) * per_home)
        block = [summed[here, h * head_dim : (h + 1) * head_dim] for h in range(heads)]
        out_ref[g] = jnp.concatenate(
            block + [marks[here]], axis=0
        ).astype(BF16)


def project_kernel(part_ref, state_ref, weight_ref, out_ref):
    sources, rows, head_dim = part_ref.shape
    blocks, req, own = out_ref.shape
    heads = rows // req - 1
    fresh = state_ref[:, head_dim:]
    parts = [part_ref[s].astype(F32) for s in range(sources)]
    points = [part[heads * req :] for part in parts]
    peak = fresh
    for point in points:
        peak = jnp.maximum(peak, point)
    weight = jnp.exp(fresh - peak)
    total = weight
    summed = [weight[:, h : h + 1] * state_ref[:, :head_dim] for h in range(heads)]
    for part, point in zip(parts, points):
        factor = jnp.exp(point - peak)
        addends = pltpu.roll(point, LANES - heads, 1) + pltpu.roll(point, LANES - 2 * heads, 1)
        total = total + factor * addends
        for h in range(heads):
            summed[h] = summed[h] + factor[:, h : h + 1] * part[h * req : (h + 1) * req]
    given = jnp.concatenate(
        [summed[h] / total[:, h : h + 1] for h in range(heads)], axis=1
    ).astype(BF16)
    for k in range(blocks):
        out_ref[k] = jnp.dot(
            given, weight_ref[:, k * own : (k + 1) * own], preferred_element_type=F32
        ).astype(BF16)


def body(n_dp, n_tensor, queries, new_kv, kv_pages, lengths, page_table, out_weight):
    req_home, q_width = queries.shape
    _, pool_home, page_len, width = kv_pages.shape
    head_dim = width // 2
    heads = q_width // head_dim
    list_len = page_table.shape[1]
    features = out_weight.shape[1]
    requests = req_home * n_dp
    scaling = head_dim ** (-0.5)

    vmem = pl.BlockSpec(memory_space=pltpu.VMEM)
    begun = pl.pallas_call(
        begin_kernel,
        out_shape=jax.ShapeDtypeStruct((8, LANES), jnp.int32),
        out_specs=vmem,
        compiler_params=pltpu.CompilerParams(vmem_limit_bytes=2**20),
        cost_estimate=pl.CostEstimate(flops=10**10, bytes_accessed=2**20, transcendentals=0),
        name="begin",
    )()
    asked, state = pl.pallas_call(
        functools.partial(ask_kernel, scaling, page_len),
        out_shape=(
            jax.ShapeDtypeStruct((n_dp, req_home, q_width + 2 * list_len), BF16),
            jax.ShapeDtypeStruct((req_home, width), F32),
        ),
        in_specs=[vmem] * 5,
        out_specs=(vmem, vmem),
        compiler_params=pltpu.CompilerParams(vmem_limit_bytes=4 * 2**20),
        cost_estimate=pl.CostEstimate(flops=10**11, bytes_accessed=2**20, transcendentals=0),
        name="ask",
    )(begun, lengths.reshape(1, req_home), queries, new_kv[:, 0, :], page_table)
    asked = lax.all_to_all(asked, "dp", 0, 0).reshape(requests, q_width + 2 * list_len)
    parts = pl.pallas_call(
        functools.partial(attend_kernel, scaling, n_dp, heads),
        out_shape=jax.ShapeDtypeStruct((n_dp, req_home * (heads + 1), head_dim), BF16),
        in_specs=[vmem] * 2,
        out_specs=vmem,
        compiler_params=pltpu.CompilerParams(vmem_limit_bytes=12 * 2**20),
        cost_estimate=pl.CostEstimate(flops=10**10, bytes_accessed=2**22, transcendentals=0),
        name="attend",
    )(asked, kv_pages[0])
    parts = lax.all_to_all(parts, "dp", 0, 0)

    own = features // n_tensor
    partial_out = pl.pallas_call(
        project_kernel,
        out_shape=jax.ShapeDtypeStruct((n_tensor, req_home, own), BF16),
        in_specs=[vmem] * 3,
        out_specs=vmem,
        compiler_params=pltpu.CompilerParams(vmem_limit_bytes=24 * 2**20),
        cost_estimate=pl.CostEstimate(flops=10**9, bytes_accessed=2**24, transcendentals=0),
        name="project",
    )(parts, state, out_weight)

    pieces = lax.all_to_all(partial_out, "tensor", 0, 0)
    return jnp.sum(pieces.astype(F32), axis=0).astype(BF16)


def solution(mesh):
    return jax.shard_map(
        functools.partial(body, mesh.shape["dp"], mesh.shape["tensor"]),
        mesh=mesh,
        in_specs=(
            P("dp", "tensor"),
            P("dp", "tensor", None),
            P("tensor", "dp", None, None),
            P("dp"),
            P("dp", None),
            P("tensor", None),
        ),
        out_specs=P("dp", "tensor"),
        check_vma=False,
    )
```

```python
import functools

import jax
import jax.numpy as jnp
from jax import lax
from jax.experimental import pallas as pl
from jax.experimental.pallas import tpu as pltpu
from jax.sharding import PartitionSpec as P

FAR_BELOW = -1e30
LANES = 128
F32 = jnp.float32
BF16 = jnp.bfloat16
PAGE_SHIFT = 256
NO_PAGE = 1024.0
CORES = 2
GROUP = 8


def iota(shape, axis):
    return lax.broadcasted_iota(jnp.int32, shape, axis)


def begin_kernel(out_ref):
    out_ref[...] = jnp.zeros_like(out_ref)


def ask_kernel(
    scaling, page_len, _, length_ref, query_ref, newest_ref, table_ref, asked_ref, state_ref
):
    req, q_width = query_ref.shape
    list_len = table_ref.shape[1]
    head_dim = newest_ref.shape[1] // 2
    heads = q_width // head_dim
    length = jnp.broadcast_to(length_ref[...], (req, req))
    length = jnp.where(iota((req, req), 0) == iota((req, req), 1), length, 0).astype(F32)
    length = jnp.sum(length, axis=1, keepdims=True)
    first = (iota((req, list_len), 1) * page_len).astype(F32)
    query = query_ref[...]
    named = (table_ref[...] - PAGE_SHIFT).astype(F32).astype(BF16)
    filled = jnp.clip(length - first, 0.0, float(page_len)).astype(BF16)
    asked_ref[:, :q_width] = query
    asked_ref[:, q_width : q_width + list_len] = named
    asked_ref[:, q_width + list_len :] = filled
    newest = newest_ref[...].astype(F32)
    wide = query.astype(F32)
    fresh = jnp.zeros((req, LANES), F32)
    for h in range(heads):
        product = wide[:, h * head_dim : (h + 1) * head_dim] * newest[:, :head_dim]
        score = jnp.sum(product, axis=1, keepdims=True) * scaling
        fresh = jnp.where(iota((req, LANES), 1) == h, score, fresh)
    state_ref[:, :head_dim] = newest[:, head_dim:]
    state_ref[:, head_dim:] = fresh


def turn_kernel(kv_ref, out_ref):
    for p in range(kv_ref.shape[0]):
        out_ref[p] = kv_ref[p, :, : out_ref.shape[1]].T


def attend_kernel(scaling, homes, heads, chip_ref, *refs):
    *other_refs, turned_ref, kv_ref, out_ref = refs
    asked_refs = (chip_ref, *other_refs)
    pages, page_len, width = kv_ref.shape
    head_dim = width // 2
    per_chip = chip_ref.shape[0]
    requests = per_chip * len(asked_refs)
    per_home = requests // homes
    q_width = heads * head_dim

    page_id = iota((pages, LANES), 0).astype(F32) + (
        lax.axis_index("dp") * pages - PAGE_SHIFT
    ).astype(F32)
    found = jnp.zeros((pages, LANES), F32)
    for k, asked_ref in enumerate(asked_refs):
        filled = asked_ref[:, q_width + LANES : q_width + 2 * LANES].astype(F32)
        named = asked_ref[:, q_width : q_width + LANES].astype(F32)
        named = jnp.where(filled > 0.0, named, NO_PAGE)
        coded = filled + (iota(filled.shape, 0) + k * per_chip).astype(F32) * 256.0
        for r in range(per_chip):
            found = jnp.where(named[r : r + 1, :] == page_id, coded[r : r + 1, :], found)
    code = jnp.broadcast_to(jnp.sum(found, axis=1, keepdims=True), (pages, LANES))
    owner = jnp.floor(code * (1.0 / 256.0))
    alive = iota((pages, page_len), 1).astype(F32) < code - owner * 256.0
    owns = owner == iota((pages, LANES), 1).astype(F32)
    picker = jnp.where(owns, 1.0, 0.0)

    asked = jnp.concatenate([ref[:, :q_width] for ref in asked_refs], axis=0)
    picked = jnp.dot(picker[:, :requests].astype(BF16), asked, preferred_element_type=F32)
    query = [picked[:, h * head_dim : (h + 1) * head_dim] for h in range(heads)]

    member = iota((GROUP, LANES), 0)
    scores = [[] for _ in range(heads)]
    for j in range(pages // GROUP):
        here = slice(j * GROUP, (j + 1) * GROUP)
        asking = jnp.concatenate(
            [
                jnp.concatenate(
                    [jnp.where(member == g, query[h][here], 0.0) for g in range(GROUP)], axis=1
                )
                for h in range(heads)
            ],
            axis=0,
        ).astype(BF16)
        group_scores = jnp.dot(
            asking,
            turned_ref[here].reshape(GROUP * head_dim, page_len),
            preferred_element_type=F32,
        )
        for h in range(heads):
            scores[h].append(group_scores[h * GROUP : (h + 1) * GROUP])
    page_peak, page_total, local = [], [], []
    for h in range(heads):
        score = jnp.where(alive, jnp.concatenate(scores[h], axis=0) * scaling, FAR_BELOW)
        page_peak.append(jnp.max(score, axis=1, keepdims=True))
        local.append(jnp.where(alive, jnp.exp(score - page_peak[h]), 0.0))
        page_total.append(jnp.sum(local[h], axis=1, keepdims=True))
    values = [[] for _ in range(heads)]
    for j in range(pages // GROUP):
        here = slice(j * GROUP, (j + 1) * GROUP)
        weights = jnp.concatenate(
            [
                jnp.concatenate(
                    [jnp.where(member == g, local[h][here], 0.0) for g in range(GROUP)], axis=1
                )
                for h in range(heads)
            ],
            axis=0,
        ).astype(BF16)
        group_values = jnp.dot(
            weights,
            kv_ref[here, :, head_dim:].reshape(GROUP * page_len, head_dim),
            preferred_element_type=F32,
        )
        for h in range(heads):
            values[h].append(group_values[h * GROUP : (h + 1) * GROUP])

    points, totals, scaled = [], [], []
    for h in range(heads):
        peak = jnp.max(jnp.where(owns, page_peak[h], FAR_BELOW), axis=0, keepdims=True)
        point = peak.astype(BF16).astype(F32)
        shift = jnp.max(jnp.where(owns, point, FAR_BELOW), axis=1, keepdims=True)
        factor = jnp.exp(jnp.minimum(page_peak[h] - shift, 80.0))
        total = jnp.sum(jnp.where(owns, page_total[h] * factor, 0.0), axis=0, keepdims=True)
        points.append(point)
        totals.append(total)
        scaled.append(jnp.concatenate(values[h], axis=0) * factor)
    scaled = jnp.concatenate(scaled, axis=1)
    high = scaled.astype(BF16)
    low = (scaled - high.astype(F32)).astype(BF16)
    chosen = picker.T[:requests].astype(BF16)
    summed = jnp.dot(chosen, high, preferred_element_type=F32) + jnp.dot(
        chosen, low, preferred_element_type=F32
    )
    high = [total.astype(BF16).astype(F32) for total in totals]
    low = [total - part for total, part in zip(totals, high)]
    marks = jnp.concatenate(points + high + low + low, axis=0).T[:requests]
    marks = jnp.concatenate([marks, jnp.zeros((requests, LANES - 4 * heads), F32)], axis=1)
    for g in range(requests // per_home):
        here = slice(g * per_home, (g + 1) * per_home)
        block = [summed[here, h * head_dim : (h + 1) * head_dim] for h in range(heads)]
        core, chip = divmod(g, homes // CORES)
        out_ref[lax.axis_index("dp") ^ (chip * CORES + core)] = jnp.concatenate(
            block + [marks[here]], axis=0
        ).astype(BF16)


def project_kernel(part_ref, state_ref, weight_ref, out_ref):
    sources, rows, head_dim = part_ref.shape
    blocks, req, own = out_ref.shape
    heads = rows // req - 1
    fresh = state_ref[:, head_dim:]
    parts = [part_ref[s].astype(F32) for s in range(sources)]
    points = [part[heads * req :] for part in parts]
    peak = fresh
    for point in points:
        peak = jnp.maximum(peak, point)
    weight = jnp.exp(fresh - peak)
    total = weight
    summed = [weight[:, h : h + 1] * state_ref[:, :head_dim] for h in range(heads)]
    for part, point in zip(parts, points):
        factor = jnp.exp(point - peak)
        addends = pltpu.roll(point, LANES - heads, 1) + pltpu.roll(point, LANES - 2 * heads, 1)
        total = total + factor * addends
        for h in range(heads):
            summed[h] = summed[h] + factor[:, h : h + 1] * part[h * req : (h + 1) * req]
    given = jnp.concatenate(
        [summed[h] / total[:, h : h + 1] for h in range(heads)], axis=1
    ).astype(BF16)
    for k in range(blocks):
        out_ref[k] = jnp.dot(
            given, weight_ref[:, k * own : (k + 1) * own], preferred_element_type=F32
        ).astype(BF16)


def body(n_dp, n_tensor, queries, new_kv, kv_pages, lengths, page_table, out_weight):
    req_home, q_width = queries.shape
    _, pool_home, page_len, width = kv_pages.shape
    head_dim = width // 2
    heads = q_width // head_dim
    list_len = page_table.shape[1]
    features = out_weight.shape[1]
    requests = req_home * n_dp
    scaling = head_dim ** (-0.5)

    vmem = pl.BlockSpec(memory_space=pltpu.VMEM)
    begun = pl.pallas_call(
        begin_kernel,
        out_shape=jax.ShapeDtypeStruct((8, LANES), jnp.int32),
        out_specs=vmem,
        compiler_params=pltpu.CompilerParams(vmem_limit_bytes=2**20),
        cost_estimate=pl.CostEstimate(flops=10**10, bytes_accessed=2**20, transcendentals=0),
        name="begin",
    )()
    asked, state = pl.pallas_call(
        functools.partial(ask_kernel, scaling, page_len),
        out_shape=(
            jax.ShapeDtypeStruct((req_home, q_width + 2 * list_len), BF16),
            jax.ShapeDtypeStruct((req_home, width), F32),
        ),
        in_specs=[vmem] * 5,
        out_specs=(vmem, vmem),
        compiler_params=pltpu.CompilerParams(vmem_limit_bytes=4 * 2**20),
        cost_estimate=pl.CostEstimate(flops=10**11, bytes_accessed=2**20, transcendentals=0),
        name="ask",
    )(begun, lengths.reshape(1, req_home), queries, new_kv[:, 0, :], page_table)
    def swap(x, mask):
        return lax.ppermute(x, "dp", [(i, i ^ mask) for i in range(n_dp)])

    near = [asked] + [swap(asked, CORES * k) for k in range(1, n_dp // CORES)]
    near = jnp.concatenate(near, axis=0)
    far = swap(near, 1)
    turned = pl.pallas_call(
        turn_kernel,
        out_shape=jax.ShapeDtypeStruct((pool_home, head_dim, page_len), BF16),
        in_specs=[vmem],
        out_specs=vmem,
        compiler_params=pltpu.CompilerParams(vmem_limit_bytes=8 * 2**20),
        cost_estimate=pl.CostEstimate(flops=10**8, bytes_accessed=2**22, transcendentals=0),
        name="turn",
    )(kv_pages[0])
    parts = pl.pallas_call(
        functools.partial(attend_kernel, scaling, n_dp, heads),
        out_shape=jax.ShapeDtypeStruct((n_dp, req_home * (heads + 1), head_dim), BF16),
        in_specs=[vmem] * 4,
        out_specs=vmem,
        compiler_params=pltpu.CompilerParams(vmem_limit_bytes=12 * 2**20),
        cost_estimate=pl.CostEstimate(flops=10**10, bytes_accessed=2**22, transcendentals=0),
        name="attend",
    )(near, far, turned, kv_pages[0])
    parts = lax.all_to_all(parts, "dp", 0, 0)

    own = features // n_tensor
    partial_out = pl.pallas_call(
        project_kernel,
        out_shape=jax.ShapeDtypeStruct((n_tensor, req_home, own), BF16),
        in_specs=[vmem] * 3,
        out_specs=vmem,
        compiler_params=pltpu.CompilerParams(vmem_limit_bytes=24 * 2**20),
        cost_estimate=pl.CostEstimate(flops=10**9, bytes_accessed=2**24, transcendentals=0),
        name="project",
    )(parts, state, out_weight)

    pieces = lax.all_to_all(partial_out, "tensor", 0, 0)
    return jnp.sum(pieces.astype(F32), axis=0).astype(BF16)


def solution(mesh):
    return jax.shard_map(
        functools.partial(body, mesh.shape["dp"], mesh.shape["tensor"]),
        mesh=mesh,
        in_specs=(
            P("dp", "tensor"),
            P("dp", "tensor", None),
            P("tensor", "dp", None, None),
            P("dp"),
            P("dp", None),
            P("tensor", None),
        ),
        out_specs=P("dp", "tensor"),
        check_vma=False,
    )
```

```python
import functools

import jax
import jax.numpy as jnp
from jax import lax
from jax.experimental import pallas as pl
from jax.experimental.pallas import tpu as pltpu
from jax.sharding import PartitionSpec as P

FAR_BELOW = -1e30
LANES = 128
F32 = jnp.float32
BF16 = jnp.bfloat16
PAGE_SHIFT = 256
NO_PAGE = 1024.0
CORES = 2
GROUP = 8


def iota(shape, axis):
    return lax.broadcasted_iota(jnp.int32, shape, axis)


def begin_kernel(out_ref):
    out_ref[...] = jnp.zeros_like(out_ref)


def ask_kernel(
    scaling, page_len, _, length_ref, query_ref, newest_ref, table_ref, asked_ref, state_ref
):
    req, q_width = query_ref.shape
    list_len = table_ref.shape[1]
    head_dim = newest_ref.shape[1] // 2
    heads = q_width // head_dim
    length = jnp.broadcast_to(length_ref[...], (req, req))
    length = jnp.where(iota((req, req), 0) == iota((req, req), 1), length, 0).astype(F32)
    length = jnp.sum(length, axis=1, keepdims=True)
    first = (iota((req, list_len), 1) * page_len).astype(F32)
    query = query_ref[...]
    named = (table_ref[...] - PAGE_SHIFT).astype(F32).astype(BF16)
    filled = jnp.clip(length - first, 0.0, float(page_len)).astype(BF16)
    asked_ref[:, :q_width] = query
    asked_ref[:, q_width : q_width + list_len] = named
    asked_ref[:, q_width + list_len :] = filled
    newest = newest_ref[...].astype(F32)
    wide = query.astype(F32)
    fresh = jnp.zeros((req, LANES), F32)
    for h in range(heads):
        product = wide[:, h * head_dim : (h + 1) * head_dim] * newest[:, :head_dim]
        score = jnp.sum(product, axis=1, keepdims=True) * scaling
        fresh = jnp.where(iota((req, LANES), 1) == h, score, fresh)
    state_ref[:, :head_dim] = newest[:, head_dim:]
    state_ref[:, head_dim:] = fresh


def search(asked_ref, first, found):
    pages = found.shape[0]
    q_width = asked_ref.shape[1] - 2 * LANES
    page_id = iota((pages, LANES), 0).astype(F32) + (
        lax.axis_index("dp") * pages - PAGE_SHIFT
    ).astype(F32)
    filled = asked_ref[:, q_width + LANES : q_width + 2 * LANES].astype(F32)
    named = asked_ref[:, q_width : q_width + LANES].astype(F32)
    named = jnp.where(filled > 0.0, named, NO_PAGE)
    coded = filled + (iota(filled.shape, 0) + first).astype(F32) * 256.0
    for r in range(filled.shape[0]):
        found = jnp.where(named[r : r + 1, :] == page_id, coded[r : r + 1, :], found)
    return found


def turn_kernel(near_ref, kv_ref, out_ref, found_ref):
    for p in range(kv_ref.shape[0]):
        out_ref[p] = kv_ref[p, :, : out_ref.shape[1]].T
    found_ref[...] = search(near_ref, 0, jnp.zeros(found_ref.shape, F32))


def attend_kernel(scaling, homes, heads, chip_ref, *refs):
    *other_refs, found_ref, turned_ref, kv_ref, out_ref = refs
    asked_refs = (chip_ref, *other_refs)
    pages, page_len, width = kv_ref.shape
    head_dim = width // 2
    per_chip = chip_ref.shape[0]
    requests = per_chip * len(asked_refs)
    per_home = requests // homes
    q_width = heads * head_dim

    found = found_ref[...]
    for k, asked_ref in enumerate(other_refs):
        found = search(asked_ref, (k + 1) * per_chip, found)
    code = jnp.broadcast_to(jnp.sum(found, axis=1, keepdims=True), (pages, LANES))
    owner = jnp.floor(code * (1.0 / 256.0))
    alive = iota((pages, page_len), 1).astype(F32) < code - owner * 256.0
    owns = owner == iota((pages, LANES), 1).astype(F32)
    picker = jnp.where(owns, 1.0, 0.0)

    asked = jnp.concatenate([ref[:, :q_width] for ref in asked_refs], axis=0)
    picked = jnp.dot(picker[:, :requests].astype(BF16), asked, preferred_element_type=F32)
    query = [picked[:, h * head_dim : (h + 1) * head_dim] for h in range(heads)]

    member = iota((GROUP, LANES), 0)
    scores = [[] for _ in range(heads)]
    for j in range(pages // GROUP):
        here = slice(j * GROUP, (j + 1) * GROUP)
        asking = jnp.concatenate(
            [
                jnp.concatenate(
                    [jnp.where(member == g, query[h][here], 0.0) for g in range(GROUP)], axis=1
                )
                for h in range(heads)
            ],
            axis=0,
        ).astype(BF16)
        group_scores = jnp.dot(
            asking,
            turned_ref[here].reshape(GROUP * head_dim, page_len),
            preferred_element_type=F32,
        )
        for h in range(heads):
            scores[h].append(group_scores[h * GROUP : (h + 1) * GROUP])
    page_peak, page_total, local = [], [], []
    for h in range(heads):
        score = jnp.where(alive, jnp.concatenate(scores[h], axis=0) * scaling, FAR_BELOW)
        page_peak.append(jnp.max(score, axis=1, keepdims=True))
        local.append(jnp.where(alive, jnp.exp(score - page_peak[h]), 0.0))
        page_total.append(jnp.sum(local[h], axis=1, keepdims=True))
    values = [[] for _ in range(heads)]
    for j in range(pages // GROUP):
        here = slice(j * GROUP, (j + 1) * GROUP)
        weights = jnp.concatenate(
            [
                jnp.concatenate(
                    [jnp.where(member == g, local[h][here], 0.0) for g in range(GROUP)], axis=1
                )
                for h in range(heads)
            ],
            axis=0,
        ).astype(BF16)
        group_values = jnp.dot(
            weights,
            kv_ref[here, :, head_dim:].reshape(GROUP * page_len, head_dim),
            preferred_element_type=F32,
        )
        for h in range(heads):
            values[h].append(group_values[h * GROUP : (h + 1) * GROUP])

    points, totals, scaled = [], [], []
    for h in range(heads):
        peak = jnp.max(jnp.where(owns, page_peak[h], FAR_BELOW), axis=0, keepdims=True)
        point = peak.astype(BF16).astype(F32)
        shift = jnp.max(jnp.where(owns, point, FAR_BELOW), axis=1, keepdims=True)
        factor = jnp.exp(jnp.minimum(page_peak[h] - shift, 80.0))
        total = jnp.sum(jnp.where(owns, page_total[h] * factor, 0.0), axis=0, keepdims=True)
        points.append(point)
        totals.append(total)
        scaled.append(jnp.concatenate(values[h], axis=0) * factor)
    scaled = jnp.concatenate(scaled, axis=1)
    high = scaled.astype(BF16)
    low = (scaled - high.astype(F32)).astype(BF16)
    chosen = picker.T[:requests].astype(BF16)
    summed = jnp.dot(chosen, high, preferred_element_type=F32) + jnp.dot(
        chosen, low, preferred_element_type=F32
    )
    high = [total.astype(BF16).astype(F32) for total in totals]
    low = [total - part for total, part in zip(totals, high)]
    marks = jnp.concatenate(points + high + low + low, axis=0).T[:requests]
    marks = jnp.concatenate([marks, jnp.zeros((requests, LANES - 4 * heads), F32)], axis=1)
    for g in range(requests // per_home):
        here = slice(g * per_home, (g + 1) * per_home)
        block = [summed[here, h * head_dim : (h + 1) * head_dim] for h in range(heads)]
        core, chip = divmod(g, homes // CORES)
        out_ref[lax.axis_index("dp") ^ (chip * CORES + core)] = jnp.concatenate(
            block + [marks[here]], axis=0
        ).astype(BF16)


def project_kernel(part_ref, state_ref, weight_ref, out_ref):
    sources, rows, head_dim = part_ref.shape
    blocks, req, own = out_ref.shape
    heads = rows // req - 1
    fresh = state_ref[:, head_dim:]
    parts = [part_ref[s].astype(F32) for s in range(sources)]
    points = [part[heads * req :] for part in parts]
    peak = fresh
    for point in points:
        peak = jnp.maximum(peak, point)
    weight = jnp.exp(fresh - peak)
    total = weight
    summed = [weight[:, h : h + 1] * state_ref[:, :head_dim] for h in range(heads)]
    for part, point in zip(parts, points):
        factor = jnp.exp(point - peak)
        addends = pltpu.roll(point, LANES - heads, 1) + pltpu.roll(point, LANES - 2 * heads, 1)
        total = total + factor * addends
        for h in range(heads):
            summed[h] = summed[h] + factor[:, h : h + 1] * part[h * req : (h + 1) * req]
    given = jnp.concatenate(
        [summed[h] / total[:, h : h + 1] for h in range(heads)], axis=1
    ).astype(BF16)
    for k in range(blocks):
        out_ref[k] = jnp.dot(
            given, weight_ref[:, k * own : (k + 1) * own], preferred_element_type=F32
        ).astype(BF16)


def body(n_dp, n_tensor, queries, new_kv, kv_pages, lengths, page_table, out_weight):
    req_home, q_width = queries.shape
    _, pool_home, page_len, width = kv_pages.shape
    head_dim = width // 2
    heads = q_width // head_dim
    list_len = page_table.shape[1]
    features = out_weight.shape[1]
    requests = req_home * n_dp
    scaling = head_dim ** (-0.5)

    vmem = pl.BlockSpec(memory_space=pltpu.VMEM)
    begun = pl.pallas_call(
        begin_kernel,
        out_shape=jax.ShapeDtypeStruct((8, LANES), jnp.int32),
        out_specs=vmem,
        compiler_params=pltpu.CompilerParams(vmem_limit_bytes=2**20),
        cost_estimate=pl.CostEstimate(flops=10**10, bytes_accessed=2**20, transcendentals=0),
        name="begin",
    )()
    asked, state = pl.pallas_call(
        functools.partial(ask_kernel, scaling, page_len),
        out_shape=(
            jax.ShapeDtypeStruct((req_home, q_width + 2 * list_len), BF16),
            jax.ShapeDtypeStruct((req_home, width), F32),
        ),
        in_specs=[vmem] * 5,
        out_specs=(vmem, vmem),
        compiler_params=pltpu.CompilerParams(vmem_limit_bytes=4 * 2**20),
        cost_estimate=pl.CostEstimate(flops=10**11, bytes_accessed=2**20, transcendentals=0),
        name="ask",
    )(begun, lengths.reshape(1, req_home), queries, new_kv[:, 0, :], page_table)
    def swap(x, mask):
        return lax.ppermute(x, "dp", [(i, i ^ mask) for i in range(n_dp)])

    near = [asked] + [swap(asked, CORES * k) for k in range(1, n_dp // CORES)]
    near = jnp.concatenate(near, axis=0)
    far = swap(near, 1)
    turned, found = pl.pallas_call(
        turn_kernel,
        out_shape=(
            jax.ShapeDtypeStruct((pool_home, head_dim, page_len), BF16),
            jax.ShapeDtypeStruct((pool_home, LANES), F32),
        ),
        in_specs=[vmem] * 2,
        out_specs=(vmem, vmem),
        compiler_params=pltpu.CompilerParams(vmem_limit_bytes=8 * 2**20),
        cost_estimate=pl.CostEstimate(flops=10**8, bytes_accessed=2**22, transcendentals=0),
        name="turn",
    )(near, kv_pages[0])
    parts = pl.pallas_call(
        functools.partial(attend_kernel, scaling, n_dp, heads),
        out_shape=jax.ShapeDtypeStruct((n_dp, req_home * (heads + 1), head_dim), BF16),
        in_specs=[vmem] * 5,
        out_specs=vmem,
        compiler_params=pltpu.CompilerParams(vmem_limit_bytes=12 * 2**20),
        cost_estimate=pl.CostEstimate(flops=10**10, bytes_accessed=2**22, transcendentals=0),
        name="attend",
    )(near, far, found, turned, kv_pages[0])
    parts = lax.all_to_all(parts, "dp", 0, 0)

    own = features // n_tensor
    partial_out = pl.pallas_call(
        project_kernel,
        out_shape=jax.ShapeDtypeStruct((n_tensor, req_home, own), BF16),
        in_specs=[vmem] * 3,
        out_specs=vmem,
        compiler_params=pltpu.CompilerParams(vmem_limit_bytes=24 * 2**20),
        cost_estimate=pl.CostEstimate(flops=10**9, bytes_accessed=2**24, transcendentals=0),
        name="project",
    )(parts, state, out_weight)

    pieces = lax.all_to_all(partial_out, "tensor", 0, 0)
    return jnp.sum(pieces.astype(F32), axis=0).astype(BF16)


def solution(mesh):
    return jax.shard_map(
        functools.partial(body, mesh.shape["dp"], mesh.shape["tensor"]),
        mesh=mesh,
        in_specs=(
            P("dp", "tensor"),
            P("dp", "tensor", None),
            P("tensor", "dp", None, None),
            P("dp"),
            P("dp", None),
            P("tensor", None),
        ),
        out_specs=P("dp", "tensor"),
        check_vma=False,
    )
```

```python
import functools

import jax
import jax.numpy as jnp
from jax import lax
from jax.experimental import pallas as pl
from jax.experimental.pallas import tpu as pltpu
from jax.sharding import PartitionSpec as P

FAR_BELOW = -1e30
LANES = 128
F32 = jnp.float32
BF16 = jnp.bfloat16
PAGE_SHIFT = 256
NO_PAGE = 1024.0
CORES = 2
GROUP = 8


def iota(shape, axis):
    return lax.broadcasted_iota(jnp.int32, shape, axis)


def begin_kernel(out_ref):
    out_ref[...] = jnp.zeros_like(out_ref)


def ask_kernel(
    scaling, page_len, _, length_ref, query_ref, newest_ref, table_ref, asked_ref, state_ref
):
    req, q_width = query_ref.shape
    list_len = table_ref.shape[1]
    head_dim = newest_ref.shape[1] // 2
    heads = q_width // head_dim
    length = jnp.broadcast_to(length_ref[...], (req, req))
    length = jnp.where(iota((req, req), 0) == iota((req, req), 1), length, 0).astype(F32)
    length = jnp.sum(length, axis=1, keepdims=True)
    first = (iota((req, list_len), 1) * page_len).astype(F32)
    query = query_ref[...]
    named = (table_ref[...] - PAGE_SHIFT).astype(F32).astype(BF16)
    filled = jnp.clip(length - first, 0.0, float(page_len)).astype(BF16)
    asked_ref[:, :q_width] = query
    asked_ref[:, q_width : q_width + list_len] = named
    asked_ref[:, q_width + list_len :] = filled
    newest = newest_ref[...].astype(F32)
    wide = query.astype(F32)
    fresh = jnp.zeros((req, LANES), F32)
    for h in range(heads):
        product = wide[:, h * head_dim : (h + 1) * head_dim] * newest[:, :head_dim]
        score = jnp.sum(product, axis=1, keepdims=True) * scaling
        fresh = jnp.where(iota((req, LANES), 1) == h, score, fresh)
    state_ref[:, :head_dim] = newest[:, head_dim:]
    state_ref[:, head_dim:] = fresh


def turn_kernel(kv_ref, out_ref):
    for p in range(kv_ref.shape[0]):
        out_ref[p] = kv_ref[p, :, : out_ref.shape[1]].T


def attend_kernel(scaling, homes, heads, chip_ref, *refs):
    *other_refs, turned_ref, kv_ref, out_ref = refs
    asked_refs = (chip_ref, *other_refs)
    pages, page_len, width = kv_ref.shape
    head_dim = width // 2
    per_chip = chip_ref.shape[0]
    requests = per_chip * len(asked_refs)
    per_home = requests // homes
    q_width = heads * head_dim

    page_id = iota((pages, LANES), 0).astype(F32) + (
        lax.axis_index("dp") * pages - PAGE_SHIFT
    ).astype(F32)
    found = jnp.zeros((pages, LANES), F32)
    for k, asked_ref in enumerate(asked_refs):
        filled = asked_ref[:, q_width + LANES : q_width + 2 * LANES].astype(F32)
        named = asked_ref[:, q_width : q_width + LANES].astype(F32)
        named = jnp.where(filled > 0.0, named, NO_PAGE)
        coded = filled + (iota(filled.shape, 0) + k * per_chip).astype(F32) * 256.0
        for r in range(per_chip):
            found = jnp.where(named[r : r + 1, :] == page_id, coded[r : r + 1, :], found)
    code = jnp.broadcast_to(jnp.sum(found, axis=1, keepdims=True), (pages, LANES))
    owner = jnp.floor(code * (1.0 / 256.0))
    alive = iota((pages, page_len), 1).astype(F32) < code - owner * 256.0
    owns = owner == iota((pages, LANES), 1).astype(F32)
    picker = jnp.where(owns, 1.0, 0.0)

    asked = jnp.concatenate([ref[:, :q_width] for ref in asked_refs], axis=0)
    picked = jnp.dot(picker[:, :requests].astype(BF16), asked, preferred_element_type=F32)
    query = [picked[:, h * head_dim : (h + 1) * head_dim] for h in range(heads)]

    member = iota((GROUP, LANES), 0)
    scores = [[] for _ in range(heads)]
    for j in range(pages // GROUP):
        here = slice(j * GROUP, (j + 1) * GROUP)
        asking = jnp.concatenate(
            [
                jnp.concatenate(
                    [jnp.where(member == g, query[h][here], 0.0) for g in range(GROUP)], axis=1
                )
                for h in range(heads)
            ],
            axis=0,
        ).astype(BF16)
        group_scores = jnp.dot(
            asking,
            turned_ref[here].reshape(GROUP * head_dim, page_len),
            preferred_element_type=F32,
        )
        for h in range(heads):
            scores[h].append(group_scores[h * GROUP : (h + 1) * GROUP])
    page_peak, page_total, local = [], [], []
    for h in range(heads):
        score = jnp.where(alive, jnp.concatenate(scores[h], axis=0) * scaling, FAR_BELOW)
        page_peak.append(jnp.max(score, axis=1, keepdims=True))
        local.append(jnp.where(alive, jnp.exp(score - page_peak[h]), 0.0))
        page_total.append(jnp.sum(local[h], axis=1, keepdims=True))
    values = [[] for _ in range(heads)]
    for j in range(pages // GROUP):
        here = slice(j * GROUP, (j + 1) * GROUP)
        weights = jnp.concatenate(
            [
                jnp.concatenate(
                    [jnp.where(member == g, local[h][here], 0.0) for g in range(GROUP)], axis=1
                )
                for h in range(heads)
            ],
            axis=0,
        ).astype(BF16)
        group_values = jnp.dot(
            weights,
            kv_ref[here, :, head_dim:].reshape(GROUP * page_len, head_dim),
            preferred_element_type=F32,
        )
        for h in range(heads):
            values[h].append(group_values[h * GROUP : (h + 1) * GROUP])

    points, totals, scaled = [], [], []
    for h in range(heads):
        peak = jnp.max(jnp.where(owns, page_peak[h], FAR_BELOW), axis=0, keepdims=True)
        point = peak.astype(BF16).astype(F32)
        shift = jnp.max(jnp.where(owns, point, FAR_BELOW), axis=1, keepdims=True)
        factor = jnp.exp(jnp.minimum(page_peak[h] - shift, 80.0))
        total = jnp.sum(jnp.where(owns, page_total[h] * factor, 0.0), axis=0, keepdims=True)
        points.append(point)
        totals.append(total)
        scaled.append(jnp.concatenate(values[h], axis=0) * factor)
    scaled = jnp.concatenate(scaled, axis=1)
    high = scaled.astype(BF16)
    low = (scaled - high.astype(F32)).astype(BF16)
    chosen = picker.T[:requests].astype(BF16)
    summed = jnp.dot(chosen, high, preferred_element_type=F32) + jnp.dot(
        chosen, low, preferred_element_type=F32
    )
    high = [total.astype(BF16).astype(F32) for total in totals]
    low = [total - part for total, part in zip(totals, high)]
    marks = jnp.concatenate(points + high + low + low, axis=0).T[:requests]
    marks = jnp.concatenate([marks, jnp.zeros((requests, LANES - 4 * heads), F32)], axis=1)
    for g in range(requests // per_home):
        here = slice(g * per_home, (g + 1) * per_home)
        block = [summed[here, h * head_dim : (h + 1) * head_dim] for h in range(heads)]
        core, chip = divmod(g, homes // CORES)
        out_ref[lax.axis_index("dp") ^ (chip * CORES + core)] = jnp.concatenate(
            block + [marks[here]], axis=0
        ).astype(BF16)


def project_kernel(part_ref, state_ref, weight_ref, out_ref):
    sources, rows, head_dim = part_ref.shape
    blocks, req, own = out_ref.shape
    heads = rows // req - 1
    fresh = state_ref[:, head_dim:]
    parts = [part_ref[s].astype(F32) for s in range(sources)]
    points = [part[heads * req :] for part in parts]
    peak = fresh
    for point in points:
        peak = jnp.maximum(peak, point)
    weight = jnp.exp(fresh - peak)
    total = weight
    summed = [weight[:, h : h + 1] * state_ref[:, :head_dim] for h in range(heads)]
    for part, point in zip(parts, points):
        factor = jnp.exp(point - peak)
        addends = pltpu.roll(point, LANES - heads, 1) + pltpu.roll(point, LANES - 2 * heads, 1)
        total = total + factor * addends
        for h in range(heads):
            summed[h] = summed[h] + factor[:, h : h + 1] * part[h * req : (h + 1) * req]
    given = jnp.concatenate(
        [summed[h] / total[:, h : h + 1] for h in range(heads)], axis=1
    ).astype(BF16)
    for k in range(blocks):
        out_ref[k] = jnp.dot(
            given, weight_ref[:, k * own : (k + 1) * own], preferred_element_type=F32
        ).astype(BF16)


def body(n_dp, n_tensor, queries, new_kv, kv_pages, lengths, page_table, out_weight):
    req_home, q_width = queries.shape
    _, pool_home, page_len, width = kv_pages.shape
    head_dim = width // 2
    heads = q_width // head_dim
    list_len = page_table.shape[1]
    features = out_weight.shape[1]
    requests = req_home * n_dp
    scaling = head_dim ** (-0.5)

    vmem = pl.BlockSpec(memory_space=pltpu.VMEM)
    begun = pl.pallas_call(
        begin_kernel,
        out_shape=jax.ShapeDtypeStruct((8, LANES), jnp.int32),
        out_specs=vmem,
        compiler_params=pltpu.CompilerParams(vmem_limit_bytes=2**20),
        cost_estimate=pl.CostEstimate(flops=10**10, bytes_accessed=2**20, transcendentals=0),
        name="begin",
    )()
    asked, state = pl.pallas_call(
        functools.partial(ask_kernel, scaling, page_len),
        out_shape=(
            jax.ShapeDtypeStruct((req_home, q_width + 2 * list_len), BF16),
            jax.ShapeDtypeStruct((req_home, width), F32),
        ),
        in_specs=[vmem] * 5,
        out_specs=(vmem, vmem),
        compiler_params=pltpu.CompilerParams(vmem_limit_bytes=4 * 2**20),
        cost_estimate=pl.CostEstimate(flops=10**11, bytes_accessed=2**20, transcendentals=0),
        name="ask",
    )(begun, lengths.reshape(1, req_home), queries, new_kv[:, 0, :], page_table)
    def swap(x, mask):
        return lax.ppermute(x, "dp", [(i, i ^ mask) for i in range(n_dp)])

    moved = {k: swap(asked, CORES * k) for k in (3,2,1)}
    near = [asked] + [moved[k] for k in range(1, n_dp // CORES)]
    near = jnp.concatenate(near, axis=0)
    far = swap(near, 1)
    turned = pl.pallas_call(
        turn_kernel,
        out_shape=jax.ShapeDtypeStruct((pool_home, head_dim, page_len), BF16),
        in_specs=[vmem],
        out_specs=vmem,
        compiler_params=pltpu.CompilerParams(vmem_limit_bytes=8 * 2**20),
        cost_estimate=pl.CostEstimate(flops=10**8, bytes_accessed=2**22, transcendentals=0),
        name="turn",
    )(kv_pages[0])
    parts = pl.pallas_call(
        functools.partial(attend_kernel, scaling, n_dp, heads),
        out_shape=jax.ShapeDtypeStruct((n_dp, req_home * (heads + 1), head_dim), BF16),
        in_specs=[vmem] * 4,
        out_specs=vmem,
        compiler_params=pltpu.CompilerParams(vmem_limit_bytes=12 * 2**20),
        cost_estimate=pl.CostEstimate(flops=10**10, bytes_accessed=2**22, transcendentals=0),
        name="attend",
    )(near, far, turned, kv_pages[0])
    parts = lax.all_to_all(parts, "dp", 0, 0)

    own = features // n_tensor
    partial_out = pl.pallas_call(
        project_kernel,
        out_shape=jax.ShapeDtypeStruct((n_tensor, req_home, own), BF16),
        in_specs=[vmem] * 3,
        out_specs=vmem,
        compiler_params=pltpu.CompilerParams(vmem_limit_bytes=24 * 2**20),
        cost_estimate=pl.CostEstimate(flops=10**9, bytes_accessed=2**24, transcendentals=0),
        name="project",
    )(parts, state, out_weight)

    pieces = lax.all_to_all(partial_out, "tensor", 0, 0)
    return jnp.sum(pieces.astype(F32), axis=0).astype(BF16)


def solution(mesh):
    return jax.shard_map(
        functools.partial(body, mesh.shape["dp"], mesh.shape["tensor"]),
        mesh=mesh,
        in_specs=(
            P("dp", "tensor"),
            P("dp", "tensor", None),
            P("tensor", "dp", None, None),
            P("dp"),
            P("dp", None),
            P("tensor", None),
        ),
        out_specs=P("dp", "tensor"),
        check_vma=False,
    )
```

```python
import functools

import jax
import jax.numpy as jnp
from jax import lax
from jax.experimental import pallas as pl
from jax.experimental.pallas import tpu as pltpu
from jax.sharding import PartitionSpec as P

FAR_BELOW = -1e30
LANES = 128
F32 = jnp.float32
BF16 = jnp.bfloat16
PAGE_SHIFT = 256
NO_PAGE = 1024.0
CORES = 2
GROUP = 8


def iota(shape, axis):
    return lax.broadcasted_iota(jnp.int32, shape, axis)


def begin_kernel(out_ref):
    out_ref[...] = jnp.zeros_like(out_ref)


def ask_kernel(
    scaling, page_len, _, length_ref, query_ref, newest_ref, table_ref, asked_ref, state_ref
):
    req, q_width = query_ref.shape
    list_len = table_ref.shape[1]
    head_dim = newest_ref.shape[1] // 2
    heads = q_width // head_dim
    length = jnp.broadcast_to(length_ref[...], (req, req))
    length = jnp.where(iota((req, req), 0) == iota((req, req), 1), length, 0).astype(F32)
    length = jnp.sum(length, axis=1, keepdims=True)
    first = (iota((req, list_len), 1) * page_len).astype(F32)
    query = query_ref[...]
    named = (table_ref[...] - PAGE_SHIFT).astype(F32).astype(BF16)
    filled = jnp.clip(length - first, 0.0, float(page_len)).astype(BF16)
    asked_ref[:, :q_width] = query
    asked_ref[:, q_width : q_width + list_len] = named
    asked_ref[:, q_width + list_len :] = filled
    newest = newest_ref[...].astype(F32)
    wide = query.astype(F32)
    fresh = jnp.zeros((req, LANES), F32)
    for h in range(heads):
        product = wide[:, h * head_dim : (h + 1) * head_dim] * newest[:, :head_dim]
        score = jnp.sum(product, axis=1, keepdims=True) * scaling
        fresh = jnp.where(iota((req, LANES), 1) == h, score, fresh)
    state_ref[:, :head_dim] = newest[:, head_dim:]
    state_ref[:, head_dim:] = fresh


def turn_kernel(kv_ref, out_ref):
    for p in range(kv_ref.shape[0]):
        out_ref[p] = kv_ref[p, :, : out_ref.shape[1]].T


def attend_kernel(scaling, homes, heads, chip_ref, *refs):
    *other_refs, turned_ref, kv_ref, out_ref = refs
    asked_refs = (chip_ref, *other_refs)
    pages, page_len, width = kv_ref.shape
    head_dim = width // 2
    per_chip = chip_ref.shape[0]
    requests = per_chip * len(asked_refs)
    per_home = requests // homes
    q_width = heads * head_dim

    page_id = iota((pages, LANES), 0).astype(F32) + (
        lax.axis_index("dp") * pages - PAGE_SHIFT
    ).astype(F32)
    found = jnp.zeros((pages, LANES), F32)
    for k, asked_ref in enumerate(asked_refs):
        filled = asked_ref[:, q_width + LANES : q_width + 2 * LANES].astype(F32)
        named = asked_ref[:, q_width : q_width + LANES].astype(F32)
        named = jnp.where(filled > 0.0, named, NO_PAGE)
        coded = filled + (iota(filled.shape, 0) + k * per_chip).astype(F32) * 256.0
        for r in range(per_chip):
            found = jnp.where(named[r : r + 1, :] == page_id, coded[r : r + 1, :], found)
    code = jnp.broadcast_to(jnp.sum(found, axis=1, keepdims=True), (pages, LANES))
    owner = jnp.floor(code * (1.0 / 256.0))
    alive = iota((pages, page_len), 1).astype(F32) < code - owner * 256.0
    owns = owner == iota((pages, LANES), 1).astype(F32)
    picker = jnp.where(owns, 1.0, 0.0)

    asked = jnp.concatenate([ref[:, :q_width] for ref in asked_refs], axis=0)
    picked = jnp.dot(picker[:, :requests].astype(BF16), asked, preferred_element_type=F32)
    query = [picked[:, h * head_dim : (h + 1) * head_dim] for h in range(heads)]

    member = iota((GROUP, LANES), 0)
    scores = [[] for _ in range(heads)]
    for j in range(pages // GROUP):
        here = slice(j * GROUP, (j + 1) * GROUP)
        asking = jnp.concatenate(
            [
                jnp.concatenate(
                    [jnp.where(member == g, query[h][here], 0.0) for g in range(GROUP)], axis=1
                )
                for h in range(heads)
            ],
            axis=0,
        ).astype(BF16)
        group_scores = jnp.dot(
            asking,
            turned_ref[here].reshape(GROUP * head_dim, page_len),
            preferred_element_type=F32,
        )
        for h in range(heads):
            scores[h].append(group_scores[h * GROUP : (h + 1) * GROUP])
    page_peak, page_total, local = [], [], []
    for h in range(heads):
        score = jnp.where(alive, jnp.concatenate(scores[h], axis=0) * scaling, FAR_BELOW)
        page_peak.append(jnp.max(score, axis=1, keepdims=True))
        local.append(jnp.where(alive, jnp.exp(score - page_peak[h]), 0.0))
        page_total.append(jnp.sum(local[h], axis=1, keepdims=True))
    values = [[] for _ in range(heads)]
    for j in range(pages // GROUP):
        here = slice(j * GROUP, (j + 1) * GROUP)
        weights = jnp.concatenate(
            [
                jnp.concatenate(
                    [jnp.where(member == g, local[h][here], 0.0) for g in range(GROUP)], axis=1
                )
                for h in range(heads)
            ],
            axis=0,
        ).astype(BF16)
        group_values = jnp.dot(
            weights,
            kv_ref[here, :, head_dim:].reshape(GROUP * page_len, head_dim),
            preferred_element_type=F32,
        )
        for h in range(heads):
            values[h].append(group_values[h * GROUP : (h + 1) * GROUP])

    points, totals, scaled = [], [], []
    for h in range(heads):
        peak = jnp.max(jnp.where(owns, page_peak[h], FAR_BELOW), axis=0, keepdims=True)
        point = peak.astype(BF16).astype(F32)
        shift = jnp.max(jnp.where(owns, point, FAR_BELOW), axis=1, keepdims=True)
        factor = jnp.exp(jnp.minimum(page_peak[h] - shift, 80.0))
        total = jnp.sum(jnp.where(owns, page_total[h] * factor, 0.0), axis=0, keepdims=True)
        points.append(point)
        totals.append(total)
        scaled.append(jnp.concatenate(values[h], axis=0) * factor)
    scaled = jnp.concatenate(scaled, axis=1)
    chosen = picker.T[:requests].astype(BF16)
    summed = jnp.dot(chosen, scaled.astype(BF16), preferred_element_type=F32)
    high = [total.astype(BF16).astype(F32) for total in totals]
    low = [total - part for total, part in zip(totals, high)]
    marks = jnp.concatenate(points + high + low + low, axis=0).T[:requests]
    marks = jnp.concatenate([marks, jnp.zeros((requests, LANES - 4 * heads), F32)], axis=1)
    for g in range(requests // per_home):
        here = slice(g * per_home, (g + 1) * per_home)
        block = [summed[here, h * head_dim : (h + 1) * head_dim] for h in range(heads)]
        core, chip = divmod(g, homes // CORES)
        out_ref[lax.axis_index("dp") ^ (chip * CORES + core)] = jnp.concatenate(
            block + [marks[here]], axis=0
        ).astype(BF16)


def project_kernel(part_ref, state_ref, weight_ref, out_ref):
    sources, rows, head_dim = part_ref.shape
    blocks, req, own = out_ref.shape
    heads = rows // req - 1
    fresh = state_ref[:, head_dim:]
    parts = [part_ref[s].astype(F32) for s in range(sources)]
    points = [part[heads * req :] for part in parts]
    peak = fresh
    for point in points:
        peak = jnp.maximum(peak, point)
    weight = jnp.exp(fresh - peak)
    total = weight
    summed = [weight[:, h : h + 1] * state_ref[:, :head_dim] for h in range(heads)]
    for part, point in zip(parts, points):
        factor = jnp.exp(point - peak)
        addends = pltpu.roll(point, LANES - heads, 1) + pltpu.roll(point, LANES - 2 * heads, 1)
        total = total + factor * addends
        for h in range(heads):
            summed[h] = summed[h] + factor[:, h : h + 1] * part[h * req : (h + 1) * req]
    given = jnp.concatenate(
        [summed[h] / total[:, h : h + 1] for h in range(heads)], axis=1
    ).astype(BF16)
    for k in range(blocks):
        out_ref[k] = jnp.dot(
            given, weight_ref[:, k * own : (k + 1) * own], preferred_element_type=F32
        ).astype(BF16)


def body(n_dp, n_tensor, queries, new_kv, kv_pages, lengths, page_table, out_weight):
    req_home, q_width = queries.shape
    _, pool_home, page_len, width = kv_pages.shape
    head_dim = width // 2
    heads = q_width // head_dim
    list_len = page_table.shape[1]
    features = out_weight.shape[1]
    requests = req_home * n_dp
    scaling = head_dim ** (-0.5)

    vmem = pl.BlockSpec(memory_space=pltpu.VMEM)
    begun = pl.pallas_call(
        begin_kernel,
        out_shape=jax.ShapeDtypeStruct((8, LANES), jnp.int32),
        out_specs=vmem,
        compiler_params=pltpu.CompilerParams(vmem_limit_bytes=2**20),
        cost_estimate=pl.CostEstimate(flops=10**10, bytes_accessed=2**20, transcendentals=0),
        name="begin",
    )()
    asked, state = pl.pallas_call(
        functools.partial(ask_kernel, scaling, page_len),
        out_shape=(
            jax.ShapeDtypeStruct((req_home, q_width + 2 * list_len), BF16),
            jax.ShapeDtypeStruct((req_home, width), F32),
        ),
        in_specs=[vmem] * 5,
        out_specs=(vmem, vmem),
        compiler_params=pltpu.CompilerParams(vmem_limit_bytes=4 * 2**20),
        cost_estimate=pl.CostEstimate(flops=10**11, bytes_accessed=2**20, transcendentals=0),
        name="ask",
    )(begun, lengths.reshape(1, req_home), queries, new_kv[:, 0, :], page_table)
    def swap(x, mask):
        return lax.ppermute(x, "dp", [(i, i ^ mask) for i in range(n_dp)])

    near = [asked] + [swap(asked, CORES * k) for k in range(1, n_dp // CORES)]
    near = jnp.concatenate(near, axis=0)
    far = swap(near, 1)
    turned = pl.pallas_call(
        turn_kernel,
        out_shape=jax.ShapeDtypeStruct((pool_home, head_dim, page_len), BF16),
        in_specs=[vmem],
        out_specs=vmem,
        compiler_params=pltpu.CompilerParams(vmem_limit_bytes=8 * 2**20),
        cost_estimate=pl.CostEstimate(flops=10**8, bytes_accessed=2**22, transcendentals=0),
        name="turn",
    )(kv_pages[0])
    parts = pl.pallas_call(
        functools.partial(attend_kernel, scaling, n_dp, heads),
        out_shape=jax.ShapeDtypeStruct((n_dp, req_home * (heads + 1), head_dim), BF16),
        in_specs=[vmem] * 4,
        out_specs=vmem,
        compiler_params=pltpu.CompilerParams(vmem_limit_bytes=12 * 2**20),
        cost_estimate=pl.CostEstimate(flops=10**10, bytes_accessed=2**22, transcendentals=0),
        name="attend",
    )(near, far, turned, kv_pages[0])
    parts = lax.all_to_all(parts, "dp", 0, 0)

    own = features // n_tensor
    partial_out = pl.pallas_call(
        project_kernel,
        out_shape=jax.ShapeDtypeStruct((n_tensor, req_home, own), BF16),
        in_specs=[vmem] * 3,
        out_specs=vmem,
        compiler_params=pltpu.CompilerParams(vmem_limit_bytes=24 * 2**20),
        cost_estimate=pl.CostEstimate(flops=10**9, bytes_accessed=2**24, transcendentals=0),
        name="project",
    )(parts, state, out_weight)

    pieces = lax.all_to_all(partial_out, "tensor", 0, 0)
    return jnp.sum(pieces.astype(F32), axis=0).astype(BF16)


def solution(mesh):
    return jax.shard_map(
        functools.partial(body, mesh.shape["dp"], mesh.shape["tensor"]),
        mesh=mesh,
        in_specs=(
            P("dp", "tensor"),
            P("dp", "tensor", None),
            P("tensor", "dp", None, None),
            P("dp"),
            P("dp", None),
            P("tensor", None),
        ),
        out_specs=P("dp", "tensor"),
        check_vma=False,
    )
```
